256 devices in a mesh: seq: 8 (over y, core), expert: 32 (over z, x).
Axes of the slice: x: 4, y: 4, z: 8, core: 2. Of those that a mesh axis runs over, the one named last changes fastest.
Arguments:
- latents: bfloat16 [32768, 1536], P(('seq', 'expert')), may hold values from -6 to 6
- control: bfloat16 [32768, 1536], P(('seq', 'expert')), may hold values from -6 to 6
- control_scale: float32 [1536], replicated, may hold values from 0.1 to 1.5
- norm_gain: float32 [1536], replicated, may hold values from 0.5 to 1.5
- expert_ids: int32 [32768, 2], P(('seq', 'expert')), may hold values from 0 to 31, as said below
- gate_weights: float32 [32768, 2], P(('seq', 'expert')), may hold values from 0.1 to 1
- expert_in: bfloat16 [32, 1536, 4096], P('expert', None, 'seq'), may hold values from -0.15625 to 0.15625
- expert_out: bfloat16 [32, 4096, 1536], P('expert', 'seq'), may hold values from -0.09375 to 0.09375
- out_grad: bfloat16 [32768, 1536], P(('seq', 'expert')), may hold values from -6 to 6
Outputs:
- output: bfloat16 [32768, 1536], P(('seq', 'expert'))
- grad_latents: bfloat16 [32768, 1536], P(('seq', 'expert'))
- grad_control: bfloat16 [32768, 1536], P(('seq', 'expert'))
- grad_scale: float32 [1536], replicated
The draws below stay inside these ranges and needn't reach their ends.
Inputs may be any that keep to these rules, and one draw needn't show every extreme that they name: `expert_ids`: the 2 experts of a token differ. On the rows of one device, 4 experts are named 24 times each, 8 are not named, and every other expert is named 2 * 128 // 32 times. In each aligned block of 4096 rows every expert is named exactly 2 * 128 times.
All inputs are finite; a program needn't handle non-finite values.
Results may differ from the reference program's by a relative error of at most 0.004.
Values may be sent and summed in bfloat16 or wider, within the bound.
A program may use at most 128 MiB of HBM per device.

```python
import math
import jax
import jax.numpy as jnp
from jax import lax

D = 1536
FF = 4096
TOP = 2
TOK_DEV = 128
EXPERTS = 32
TOKENS = 32768
N_SEQ = 8
N_EXPERT = 32


def expert_order(subkey):
    return jax.random.permutation(subkey, EXPERTS)


def token_order(subkey):
    return jax.random.permutation(subkey, TOK_DEV)


def draw_expert_ids(key, part):
    key = jax.random.fold_in(key, 7)
    mean_load = TOP * TOK_DEV // EXPERTS
    heavy = EXPERTS // 8
    empty = EXPERTS // 4
    loads = jnp.concatenate([jnp.full((heavy,), 3 * mean_load, jnp.int32), jnp.zeros((empty,), jnp.int32), jnp.full((EXPERTS - heavy - empty,), mean_load, jnp.int32)])
    blocks = N_SEQ * N_EXPERT
    key_place, key_shift, key_order, key_flip = jax.random.split(key, 4)
    placing = jax.vmap(expert_order)(jax.random.split(key_place, N_SEQ))
    shifting = jax.vmap(expert_order)(jax.random.split(key_shift, N_SEQ))
    labels = jnp.arange(EXPERTS, dtype=jnp.int32)
    turned = (labels[None, None, :] + shifting[:, :, None]) % EXPERTS
    spread = jnp.broadcast_to(placing[:, None, :], turned.shape)
    slot_of = jnp.take_along_axis(spread, turned, axis=2)
    counts = loads[slot_of].reshape(blocks, EXPERTS)
    bounds = jnp.cumsum(counts, axis=1)
    spots = jnp.arange(TOP * TOK_DEV, dtype=jnp.int32)
    listed = jnp.sum((spots[None, :, None] >= bounds[:, None, :]).astype(jnp.int32), axis=2)
    pairs = jnp.stack([listed[:, :TOK_DEV], listed[:, TOK_DEV:]], axis=2)
    shuffle = jax.vmap(token_order)(jax.random.split(key_order, blocks))
    pairs = jnp.take_along_axis(pairs, shuffle[:, :, None], axis=1)
    flips = jax.random.randint(key_flip, (blocks, TOK_DEV, 1), 0, 2)
    pairs = jnp.where(flips == 1, pairs[:, :, ::-1], pairs)
    return pairs.reshape(blocks * TOK_DEV, TOP).astype(jnp.int32)


def level_of(key, shape, shards, smallest, largest):
    def one(dim, shards_of):
        draws = jax.random.uniform(jax.random.fold_in(jax.random.fold_in(key, 6), dim), (shards_of,), jnp.float32, smallest / len(shards), largest / len(shards))
        return jnp.repeat(jnp.exp(draws), shape[dim] // shards_of).reshape((-1,) + (1,) * (len(shape) - dim - 1))

    loudness = one(*shards[0])
    for cut in shards[1:]:
        loudness = loudness * one(*cut)
    return loudness


def gaussian(rng, dims, scale, bound, pieces=(), held_as=jnp.bfloat16):
    array = scale * jax.random.normal(rng, dims, jnp.float32)
    if pieces:
        array = array * level_of(rng, dims, pieces, -0.22, 0.18)
    return jnp.clip(array, -bound, bound).astype(held_as)


def setup_inputs(seed: int = 0) -> dict:
    splits = jax.random.split(jax.random.key(seed), 10)
    return {
        "latents": gaussian(splits[0], (TOKENS, D), 1.0, 6.0, ((0, 256),)),
        "control": gaussian(splits[1], (TOKENS, D), 1.0, 6.0, ((0, 256),)),
        "control_scale": jnp.clip(jnp.exp(jax.random.uniform(splits[2], (D,), jnp.float32, math.log(0.1), math.log(1.5))), 0.1, 1.5),
        "norm_gain": jnp.clip(1.0 + 0.1 * jax.random.normal(splits[3], (D,), jnp.float32), 0.5, 1.5),
        "expert_ids": draw_expert_ids(jax.random.fold_in(splits[9], 71), 0),
        "gate_weights": jnp.clip(0.1 + 0.9 * jax.random.uniform(splits[5], (TOKENS, TOP), jnp.float32) ** level_of(splits[5], (TOKENS, TOP), ((0, 256),), -0.2, 0.2), 0.1, 1.0),
        "expert_in": gaussian(splits[6], (EXPERTS, D, FF), D ** -0.5, 0.15625, ((0, 32), (2, 8))),
        "expert_out": gaussian(splits[7], (EXPERTS, FF, D), FF ** -0.5, 0.09375, ((0, 32), (1, 8))),
        "out_grad": gaussian(splits[8], (TOKENS, D), 1.0, 6.0, ((0, 256),)),
    }


coeff = 0.7978845608
cubic = 0.044715

def gelu_tanh(values):
    inner = jnp.tanh(coeff * (values + cubic * values * values * values))
    return 0.5 * values * (1.0 + inner)

def gelu_slope(values):
    inner = jnp.tanh(coeff * (values + cubic * values * values * values))
    return 0.5 * (1.0 + inner) + 0.5 * values * (1.0 - inner * inner) * coeff * (1.0 + 3.0 * cubic * values * values)

def reference(latents, control, control_scale, norm_gain, expert_ids, gate_weights, expert_in, expert_out, out_grad):
    hidden_sum = latents.astype(jnp.float32) + control_scale * control.astype(jnp.float32)
    inverse = 1.0 / jnp.sqrt(lax.optimization_barrier(jnp.mean(hidden_sum * hidden_sum, axis=-1, keepdims=True)) + 1e-06)
    normed = hidden_sum * inverse
    routed = (normed * norm_gain).astype(jnp.bfloat16)
    flat_ids = expert_ids.reshape(-1)
    sorted_at = jnp.argsort(flat_ids, stable=True).astype(jnp.int32)
    group_rows = TOKENS * TOP // EXPERTS
    owners = (sorted_at // TOP).reshape(EXPERTS, group_rows)

    def expert_pass(packed):
        owner_rows, weight_in, weight_out = packed
        in_rows = routed[owner_rows]
        grad_rows = out_grad[owner_rows]
        pre_act = jnp.dot(in_rows, weight_in, preferred_element_type=jnp.float32)
        activated = gelu_tanh(pre_act).astype(jnp.bfloat16)
        result = jnp.dot(activated, weight_out, preferred_element_type=jnp.float32).astype(jnp.bfloat16)
        slope_back = jnp.dot(grad_rows, weight_out.T, preferred_element_type=jnp.float32) * gelu_slope(pre_act)
        slope_back = slope_back.astype(jnp.bfloat16)
        input_grad = jnp.dot(slope_back, weight_in.T, preferred_element_type=jnp.float32).astype(jnp.bfloat16)
        return (result, input_grad)
    results, input_grads = lax.map(expert_pass, (owners, expert_in, expert_out))
    route_out = jnp.zeros((TOKENS * TOP, D), jnp.bfloat16).at[sorted_at].set(results.reshape(-1, D))
    route_grad = jnp.zeros((TOKENS * TOP, D), jnp.bfloat16).at[sorted_at].set(input_grads.reshape(-1, D))
    route_out = route_out.reshape(TOKENS, TOP, D).astype(jnp.float32)
    route_grad = route_grad.reshape(TOKENS, TOP, D).astype(jnp.float32)
    output = hidden_sum + lax.optimization_barrier(jnp.sum(gate_weights[:, :, None] * route_out, axis=1))
    routed_grad = lax.optimization_barrier(jnp.sum(gate_weights[:, :, None] * route_grad, axis=1))
    normed_grad = routed_grad * norm_gain
    sum_grad = inverse * (normed_grad - normed * lax.optimization_barrier(jnp.mean(normed_grad * normed, axis=-1, keepdims=True)))
    sum_grad = sum_grad + out_grad.astype(jnp.float32)
    grad_latents = sum_grad.astype(jnp.bfloat16)
    grad_control = (sum_grad * control_scale).astype(jnp.bfloat16)
    grad_scale = lax.optimization_barrier(jnp.sum(sum_grad * control.astype(jnp.float32), axis=0))
    return (output.astype(jnp.bfloat16), grad_latents, grad_control, grad_scale)
```

```python
import jax
import jax.numpy as jnp
from jax import lax
from jax.experimental import pallas as pl
from jax.experimental.pallas import tpu as pltpu
from jax.sharding import PartitionSpec as P

coeff = 0.7978845608
cubic = 0.044715

MESH = pl.DeviceIdType.MESH
BF = jnp.bfloat16
F32 = jnp.float32

T = 128
CAP = 24
PAIR = 2 * CAP
ROWS = 256
D = 1536
SH = 512
HID = 2 * SH
RES, GRAD = 0, 1
NT = 256
Z_SLOT = {1: 2, 2: 4, 3: 6, 4: 1, 5: 7, 6: 5, 7: 3}


def nn(a, b):
    return lax.dot_general(a, b, (((1,), (0,)), ((), ())), preferred_element_type=F32)


def nt(a, b):
    return lax.dot_general(a, b, (((1,), (1,)), ((), ())), preferred_element_type=F32)


def tn(a, b):
    return lax.dot_general(a, b, (((0,), (0,)), ((), ())), preferred_element_type=F32)


def iota(shape, dim):
    return lax.broadcasted_iota(jnp.int32, shape, dim)


class Wires:
    def __init__(self, send, recv):
        self.send, self.recv = send, recv
        self.copies = {}
        self.sent = set()

    def start(self, key, src, dst, device):
        place = len(self.copies)
        copy = pltpu.make_async_remote_copy(
            src_ref=src,
            dst_ref=dst,
            send_sem=self.send.at[place],
            recv_sem=self.recv.at[place],
            device_id=device,
            device_id_type=MESH,
        )
        copy.start()
        self.copies[key] = copy

    def arrived(self, key):
        self.copies[key].wait_recv()

    def left(self, key):
        if key not in self.sent:
            self.sent.add(key)
            self.copies[key].wait_send()

    def finish(self):
        for key in self.copies:
            self.left(key)


N_COPIES = 14 + 7 + 3 + 2 + 14 + 24 + 6 + 6 + 24 + 28 + 14


def kernel(
    meta_ref, lat_ref, ctl_ref, og_ref, cs_ref, ng_ref, wi_ref, wo_ref,
    out_ref, gl_ref, gc_ref, gs_ref,
    zb, xst, xsl, rows, wi, wo, act, slope, fr, fin, pb, pown, own, codes, pick, meta, hid, gb,
    send, recv, lsem, free,
):
    me_s, me_e = lax.axis_index("seq"), lax.axis_index("expert")
    y, c = lax.div(me_s, 2), lax.rem(me_s, 2)
    z, x = lax.div(me_e, 4), lax.rem(me_e, 4)

    def z_at(delta):
        return (me_s, lax.rem(z + delta + 8, 8) * 4 + x)

    def x_at(delta):
        return (me_s, z * 4 + lax.rem(x + delta + 4, 4))

    def y_at(delta):
        return (lax.rem(y + delta, 4) * 2 + c, me_e)

    odd = lax.rem(y, 2)
    sibling = (y * 2 + 1 - c, me_e)
    w_mate = ((y + 1 - 2 * odd) * 2 + c, me_e)
    t_mate = (lax.rem(y + 3 + 2 * odd, 4) * 2 + c, me_e)
    peers = [z_at(k) for k in range(1, 8)] + [x_at(k) for k in range(1, 4)]
    peers += [y_at(k) for k in range(1, 4)] + [sibling]

    barrier = pltpu.get_barrier_semaphore()
    for peer in peers:
        pl.semaphore_signal(barrier, inc=1, device_id=peer, device_id_type=MESH)

    own_in = pltpu.make_async_copy(wi_ref.at[0], wi.at[:, pl.ds(0, SH)], lsem.at[0])
    own_out = pltpu.make_async_copy(wo_ref.at[0], wo.at[pl.ds(0, SH), :], lsem.at[1])
    own_in.start()
    own_out.start()

    hidden = lat_ref[...].astype(F32) + cs_ref[...] * ctl_ref[...].astype(F32)
    hid[...] = hidden
    inverse = 1.0 / jnp.sqrt(jnp.mean(hidden * hidden, axis=-1, keepdims=True) + 1e-06)
    zb[RES, 0:T] = (hidden * inverse * ng_ref[...]).astype(BF)
    zb[GRAD, 0:T] = og_ref[...]

    id0, id1 = meta_ref[0:1], meta_ref[1:2]
    labels = iota((32, T), 0).astype(F32)
    hot0 = jnp.where(id0 == labels, 1.0, 0.0)
    hot1 = jnp.where(id1 == labels, 1.0, 0.0)
    before = jnp.where(iota((T, T), 0) < iota((T, T), 1), 1.0, 0.0).astype(BF)
    rank0 = jnp.sum(hot0 * nn(hot0.astype(BF), before), axis=0, keepdims=True)
    ahead = jnp.sum(hot0, axis=1, keepdims=True)
    rank1 = jnp.sum(hot1 * (nn(hot1.astype(BF), before) + ahead), axis=0, keepdims=True)
    line = iota((8, T), 0)
    meta[0, 0:8] = jnp.where(
        line == 0, id0 * CAP + rank0, jnp.where(line == 1, id1 * CAP + rank1, meta_ref[...])
    )

    pl.semaphore_wait(barrier, len(peers))
    wires = Wires(send, recv)

    def z_own(a):
        for h in range(2):
            for side in range(2):
                wires.start(
                    ("z", a, side, h),
                    zb.at[a, pl.ds(64 * h, 64)],
                    zb.at[a, pl.ds(256 + T * side + 64 * h, 64)],
                    z_at(1 - 2 * side),
                )

    def z_forward(a, d):
        for h in range(2):
            for side in range(2):
                wires.arrived(("z", a, side, 2 * (d - 1) + h))
                src = zb.at[a, pl.ds(256 * d + T * side + 64 * h, 64)]
                if d < 3:
                    dst = zb.at[a, pl.ds(256 * (d + 1) + T * side + 64 * h, 64)]
                    wires.start(("z", a, side, 2 * d + h), src, dst, z_at(1 - 2 * side))
                elif side == h:
                    dst = zb.at[a, pl.ds(T + 64 * h, 64)]
                    wires.start(("z", a, side, 6), src, dst, z_at(1 - 2 * side))

    def targets(g, k):
        return jnp.concatenate(
            [meta[0, pl.ds(16 * g + k, 1)], meta[0, pl.ds(16 * g + 8 + k, 1)]], axis=1
        )

    def select(a, g):
        one = jnp.where(codes[...] == targets(g, 0), 1.0, 0.0)
        one = jnp.where(codes[...] == targets(g, 1), 1.0, one).astype(BF)
        for n in range(0, D, 512):
            got = nn(one, zb[a, pl.ds(256 * g, 256), pl.ds(n, 512)]).astype(BF)
            xsl[a, pl.ds(PAIR * g, PAIR), pl.ds(n, 512)] = got[0:PAIR]
            xst[a, g, pl.ds(PAIR, 3 * PAIR), pl.ds(n, 512)] = got[PAIR:]
        for j in range(1, 4):
            wires.start(
                ("x", a, j, g),
                xst.at[a, g, pl.ds(PAIR * j, PAIR)],
                xsl.at[a, pl.ds((4 * j + g) * PAIR, PAIR)],
                x_at(j),
            )

    def compact(a):
        for j in range(1, 4):
            for g in range(4):
                wires.left(("x", a, j, g))
            pl.semaphore_signal(free.at[a], inc=1, device_id=x_at(j), device_id_type=MESH)
        for j in range(1, 4):
            for g in range(4):
                wires.arrived(("x", a, j, g))
        for n in range(0, D, 512):
            rows[a, 0:ROWS, pl.ds(n, 512)] = nn(pick[...], xsl[a, :, pl.ds(n, 512)]).astype(BF)
        wires.start(
            ("e", a, 2), rows.at[a, pl.ds(0, ROWS)], rows.at[a, pl.ds(2 * ROWS, ROWS)], t_mate
        )
        wires.start(
            ("e", a, 1), rows.at[a, pl.ds(0, ROWS)], rows.at[a, pl.ds(ROWS, ROWS)], sibling
        )

    def pass_rows(a):
        wires.arrived(("e", a, 2))
        wires.start(
            ("e", a, 3),
            rows.at[a, pl.ds(2 * ROWS, ROWS)],
            rows.at[a, pl.ds(3 * ROWS, ROWS)],
            sibling,
        )

    def half(p):
        return pl.ds(2 * ROWS * p, 2 * ROWS)

    def forward(p):
        @pl.loop(0, HID // NT)
        def _(i):
            cols = pl.ds(pl.multiple_of(i * NT, NT), NT)
            v = nn(rows[RES, half(p)], wi[:, cols])
            inner = jnp.tanh(coeff * (v + cubic * v * v * v))
            act[half(p), cols] = (0.5 * v * (1.0 + inner)).astype(BF)
            slope[half(p), cols] = 0.5 * (1.0 + inner) + 0.5 * v * (1.0 - inner * inner) * coeff * (
                1.0 + 3.0 * cubic * v * v
            )

    def result(p):
        @pl.loop(0, D // NT)
        def _(i):
            cols = pl.ds(pl.multiple_of(i * NT, NT), NT)
            zb[RES, half(p), cols] = nn(act[half(p), :], wo[:, cols]).astype(BF)

    def backward(p):
        @pl.loop(0, HID // NT)
        def _(i):
            cols = pl.ds(pl.multiple_of(i * NT, NT), NT)
            act[half(p), cols] = (nt(rows[GRAD, half(p)], wo[cols, :]) * slope[half(p), cols]).astype(BF)

    def input_grad(p):
        @pl.loop(0, D // NT)
        def _(i):
            cols = pl.ds(pl.multiple_of(i * NT, NT), NT)
            zb[GRAD, half(p), cols] = nt(act[half(p), :], wi[cols, :]).astype(BF)

    def part(a, o):
        return zb.at[a, pl.ds(ROWS * o, ROWS)]

    def part_to_sibling(a, o):
        wires.start(("f", a, o), part(a, o), fr.at[a, 2 if o == 3 else 0], sibling)

    def part_to_mate(a):
        wires.arrived(("f", a, 3))
        zb[a, pl.ds(2 * ROWS, ROWS)] = (
            zb[a, pl.ds(2 * ROWS, ROWS)].astype(F32) + fr[a, 2].astype(F32)
        ).astype(BF)
        wires.start(("f", a, 2), part(a, 2), fr.at[a, 1], t_mate)

    def give_back(a):
        wires.arrived(("f", a, 1))
        wires.arrived(("f", a, 2))
        fin[...] = (
            zb[a, 0:ROWS].astype(F32) + fr[a, 0].astype(F32) + fr[a, 1].astype(F32)
        ).astype(BF)
        for n in range(0, D, 512):
            got = tn(pick[...], fin[:, pl.ds(n, 512)]).astype(BF)
            for g in range(4):
                xst[a, g, 0:PAIR, pl.ds(n, 512)] = got[PAIR * g : PAIR * (g + 1)]
            xsl[a, pl.ds(4 * PAIR, 12 * PAIR), pl.ds(n, 512)] = got[4 * PAIR :]
        pl.semaphore_wait(free.at[a], 3)
        for g in (0, 3, 2, 1):
            for j in range(1, 4):
                wires.start(
                    ("r", a, j, g),
                    xsl.at[a, pl.ds((4 * j + g) * PAIR, PAIR)],
                    xst.at[a, g, pl.ds(PAIR * j, PAIR)],
                    x_at(-j),
                )

    def gathered(a, g):
        for j in range(1, 4):
            wires.arrived(("r", a, j, g))
        gate = jnp.where(codes[...] == targets(g, 0), targets(g, 2), 0.0)
        gate = jnp.where(codes[...] == targets(g, 1), targets(g, 3), gate)
        high = gate.astype(BF)
        low = (gate - high.astype(F32)).astype(BF)

        def columns(n):
            got = xst[a, g, :, pl.ds(n, 512)]
            return tn(high, got) + tn(low, got)

        return columns

    def z_back(a, g, side, h, m):
        src = zb_back(a, g, side, h)
        dst = pb.at[a, pl.ds(256 * (g - 1) + T * side + 64 * h, 64)]
        wires.start(("b", a, side, m), src, dst, z_at(2 * side - 1))

    def zb_back(a, g, side, h):
        if g == 4:
            return pown.at[a, pl.ds(64 * h, 64)]
        return pb.at[a, pl.ds(256 * g + T * side + 64 * h, 64)]

    def reduce_first(a):
        columns = gathered(a, 0)
        for n in range(0, D, 512):
            got = columns(n)
            own[a, :, pl.ds(n, 512)] = got[0:T]
            pown[a, :, pl.ds(n, 512)] = got[T:].astype(BF)
        z_back(a, 4, 0, 0, 0)
        z_back(a, 4, 1, 1, 0)

    def reduce_next(a, g):
        columns = gathered(a, g)
        base = 256 * g
        if g == 3:
            for side in range(2):
                wires.arrived(("b", a, side, 0))
        else:
            for side in range(2):
                for h in range(2):
                    wires.arrived(("b", a, side, 5 - 2 * g + h))
        for n in range(0, D, 512):
            got = columns(n)
            spans = ((0, 64, True), (64, 128, False), (192, 64, True)) if g == 3 else ((0, 256, True),)
            for at, size, add in spans:
                value = got[at : at + size]
                if add:
                    value = value + pb[a, pl.ds(base + at, size), pl.ds(n, 512)].astype(F32)
                pb[a, pl.ds(base + at, size), pl.ds(n, 512)] = value.astype(BF)
        for h in range(2):
            for side in range(2):
                z_back(a, g, side, h, 7 - 2 * g + h)

    def reduce_last(a):
        for side in range(2):
            for h in range(2):
                wires.arrived(("b", a, side, 5 + h))
        return own[a] + pb[a, 0:T].astype(F32) + pb[a, T:256].astype(F32)


    z_own(RES)
    for k in range(1, 8):
        wires.start(("mz", k), meta.at[0, pl.ds(0, 8)], meta.at[0, pl.ds(8 * Z_SLOT[k], 8)], z_at(k))
    wires.start(("w", 0), wi_ref.at[0], wi.at[:, pl.ds(SH, SH)], w_mate)
    wires.start(("w", 1), wo_ref.at[0], wo.at[pl.ds(SH, SH), :], w_mate)
    spot = iota((PAIR, 256), 0)
    spot = jnp.where(spot >= CAP, spot - CAP + 1024, spot)
    spot = spot - jnp.where(iota((PAIR, 256), 1) >= T, 1024, 0)
    spot = jnp.where((spot >= 0) & (spot < CAP), spot, -65536).astype(F32)
    for j in range(4):
        first = (z * 4 + lax.rem(x + j, 4)) * CAP
        codes[pl.ds(PAIR * j, PAIR)] = spot + first.astype(F32)
    for k in range(1, 8):
        wires.arrived(("mz", k))
    for j in range(1, 4):
        wires.start(("mx", j), meta.at[0], meta.at[j], x_at(j))

    for d in (1, 2, 3):
        z_forward(RES, d)
        if d == 3:
            z_own(GRAD)
        select(RES, d)
    for side in range(2):
        wires.arrived(("z", RES, side, 6))
    select(RES, 0)

    for j in range(1, 4):
        wires.arrived(("mx", j))
    marks = meta[...].reshape(256, T)
    low = (me_e * CAP).astype(F32)
    named = (marks >= low) & (marks < low + CAP) & ((iota((256, T), 0) & 7) < 2)
    named = jnp.where(named, 1.0, 0.0).astype(BF)
    counts = nt(jnp.ones((8, T), BF), named).astype(BF)
    begin = (iota((256, 4 * PAIR * 4), 0) >> 3) * CAP
    slot = iota((256, 4 * PAIR * 4), 1)
    inside = (slot >= begin) & (slot < begin + CAP)
    filled = nn(counts, jnp.where(inside, 1.0, 0.0).astype(BF))
    offset = nn(counts, jnp.where(slot >= begin + CAP, 1.0, 0.0).astype(BF))
    slot = iota((8, 4 * PAIR * 4), 1).astype(F32)
    rank = slot - CAP * jnp.floor((slot + 0.5) * (1.0 / CAP))
    place = jnp.where(rank < filled, offset + rank, -1.0)
    pick[...] = jnp.where(iota((ROWS, 4 * PAIR * 4), 0).astype(F32) == place[0:1], 1.0, 0.0).astype(BF)

    z_forward(GRAD, 1)
    compact(RES)
    select(GRAD, 1)
    z_forward(GRAD, 2)
    pass_rows(RES)
    select(GRAD, 2)
    own_in.wait()
    wires.arrived(("w", 0))
    wires.arrived(("e", RES, 1))
    forward(0)
    z_forward(GRAD, 3)
    select(GRAD, 3)
    wires.arrived(("e", RES, 3))
    forward(1)
    for side in range(2):
        wires.arrived(("z", GRAD, side, 6))
    select(GRAD, 0)
    own_out.wait()
    wires.arrived(("w", 1))
    for side in range(2):
        for m in range(7):
            wires.left(("z", RES, side, m))
    result(1)
    part_to_sibling(RES, 3)
    result(0)
    part_to_sibling(RES, 1)
    compact(GRAD)
    part_to_mate(RES)
    pass_rows(GRAD)
    wires.arrived(("e", GRAD, 1))
    backward(0)
    give_back(RES)
    wires.arrived(("e", GRAD, 3))
    backward(1)
    for side in range(2):
        for m in range(7):
            wires.left(("z", GRAD, side, m))
    input_grad(1)
    part_to_sibling(GRAD, 3)
    input_grad(0)
    part_to_sibling(GRAD, 1)
    reduce_first(RES)
    part_to_mate(GRAD)
    reduce_next(RES, 3)
    give_back(GRAD)
    reduce_next(RES, 2)
    reduce_first(GRAD)
    reduce_next(RES, 1)
    reduce_next(GRAD, 3)
    out_ref[...] = (hid[...] + reduce_last(RES)).astype(BF)
    reduce_next(GRAD, 2)
    reduce_next(GRAD, 1)

    hidden = hid[...]
    inverse = 1.0 / jnp.sqrt(jnp.mean(hidden * hidden, axis=-1, keepdims=True) + 1e-06)
    normed = hidden * inverse
    normed_grad = reduce_last(GRAD) * ng_ref[...]
    mean = jnp.mean(normed_grad * normed, axis=-1, keepdims=True)
    sum_grad = inverse * (normed_grad - normed * mean) + og_ref[...].astype(F32)
    gl_ref[...] = sum_grad.astype(BF)
    gc_ref[...] = (sum_grad * cs_ref[...]).astype(BF)

    total = jnp.sum(sum_grad * ctl_ref[...].astype(F32), axis=0, keepdims=True)
    stages = (
        (0, 8, z, [z_at(k) for k in range(1, 8)]),
        (8, 4, x, [x_at(k) for k in range(1, 4)]),
        (12, 4, y, [y_at(k) for k in range(1, 4)]),
        (16, 2, c, [sibling]),
    )
    for base, size, mine, others in stages:
        gb[base + mine] = total
        for k, other in enumerate(others):
            wires.start(("g", base, k), gb.at[base + mine], gb.at[base + mine], other)
        for k in range(len(others)):
            wires.arrived(("g", base, k))
        total = gb[base]
        for k in range(1, size):
            total = total + gb[base + k]
    gs_ref[...] = total
    wires.finish()


def body(
    latents, control, control_scale, norm_gain, expert_ids, gate_weights, expert_in, expert_out, out_grad
):
    marks = jnp.concatenate(
        [expert_ids.T.astype(F32), gate_weights.T, jnp.zeros((4, T), F32)], axis=0
    )
    vmem = pl.BlockSpec(memory_space=pltpu.VMEM)
    hbm = pl.BlockSpec(memory_space=pl.ANY)
    output, grad_latents, grad_control, grad_scale = pl.pallas_call(
        kernel,
        out_shape=(
            jax.ShapeDtypeStruct((T, D), BF),
            jax.ShapeDtypeStruct((T, D), BF),
            jax.ShapeDtypeStruct((T, D), BF),
            jax.ShapeDtypeStruct((1, D), F32),
        ),
        in_specs=[vmem] * 6 + [hbm] * 2,
        out_specs=(vmem,) * 4,
        scratch_shapes=[
            pltpu.VMEM((2, 4 * 256, D), BF),
            pltpu.VMEM((2, 4, 4 * PAIR, D), BF),
            pltpu.VMEM((2, 16 * PAIR, D), BF),
            pltpu.VMEM((2, 4 * ROWS, D), BF),
            pltpu.VMEM((D, HID), BF),
            pltpu.VMEM((HID, D), BF),
            pltpu.VMEM((4 * ROWS, HID), BF),
            pltpu.VMEM((4 * ROWS, HID), F32),
            pltpu.VMEM((2, 3, ROWS, D), BF),
            pltpu.VMEM((ROWS, D), BF),
            pltpu.VMEM((2, 4 * 256, D), BF),
            pltpu.VMEM((2, T, D), BF),
            pltpu.VMEM((2, T, D), F32),
            pltpu.VMEM((4 * PAIR, 256), F32),
            pltpu.VMEM((ROWS, 16 * PAIR), BF),
            pltpu.VMEM((4, 64, T), F32),
            pltpu.VMEM((T, D), F32),
            pltpu.VMEM((18, 1, D), F32),
            pltpu.SemaphoreType.DMA((N_COPIES,)),
            pltpu.SemaphoreType.DMA((N_COPIES,)),
            pltpu.SemaphoreType.DMA((2,)),
            pltpu.SemaphoreType.REGULAR((2,)),
        ],
        compiler_params=pltpu.CompilerParams(
            collective_id=0, has_side_effects=True, vmem_limit_bytes=63 * 1024 * 1024
        ),
    )(
        marks, latents, control, out_grad, control_scale[None, :], norm_gain[None, :],
        expert_in, expert_out,
    )
    return output, grad_latents, grad_control, grad_scale[0]


def solution(mesh):
    return jax.shard_map(
        body,
        mesh=mesh,
        in_specs=(
            P(("seq", "expert"), None),
            P(("seq", "expert"), None),
            P(),
            P(),
            P(("seq", "expert"), None),
            P(("seq", "expert"), None),
            P("expert", None, "seq"),
            P("expert", "seq", None),
            P(("seq", "expert"), None),
        ),
        out_specs=(
            P(("seq", "expert"), None),
            P(("seq", "expert"), None),
            P(("seq", "expert"), None),
            P(),
        ),
        check_vma=False,
    )
```

```python
import jax
import jax.numpy as jnp
from jax import lax
from jax.experimental import pallas as pl
from jax.experimental.pallas import tpu as pltpu
from jax.sharding import PartitionSpec as P

coeff = 0.7978845608
cubic = 0.044715

MESH = pl.DeviceIdType.MESH
BF = jnp.bfloat16
F32 = jnp.float32

T = 128
CAP = 24
PAIR = 2 * CAP
ROWS = 256
D = 1536
SH = 512
HID = 2 * SH
RES, GRAD = 0, 1
NT = 256
Q = D // 2
N_SLOT = 32 * CAP
BLOCKS = {0: (0, 0, 0, HID), 1: (2 * ROWS, 2 * ROWS, 0, SH), 2: (4 * ROWS, 2 * ROWS, SH, HID)}
Z_SLOT = {1: 2, 2: 4, 3: 6, 4: 1, 5: 7, 6: 5, 7: 3}


def nn(a, b):
    return lax.dot_general(a, b, (((1,), (0,)), ((), ())), preferred_element_type=F32)


def nt(a, b):
    return lax.dot_general(a, b, (((1,), (1,)), ((), ())), preferred_element_type=F32)


def tn(a, b):
    return lax.dot_general(a, b, (((0,), (0,)), ((), ())), preferred_element_type=F32)


def iota(shape, dim):
    return lax.broadcasted_iota(jnp.int32, shape, dim)


class Wires:
    def __init__(self, send, recv):
        self.send, self.recv = send, recv
        self.copies = {}
        self.sent = set()

    def start(self, key, src, dst, device):
        place = len(self.copies)
        copy = pltpu.make_async_remote_copy(
            src_ref=src,
            dst_ref=dst,
            send_sem=self.send.at[place],
            recv_sem=self.recv.at[place],
            device_id=device,
            device_id_type=MESH,
        )
        copy.start()
        self.copies[key] = copy

    def arrived(self, key):
        self.copies[key].wait_recv()

    def left(self, key):
        if key not in self.sent:
            self.sent.add(key)
            self.copies[key].wait_send()

    def finish(self):
        for key in self.copies:
            self.left(key)


N_COPIES = 56 + 7 + 3 + 4 + 48 + 20 + 20 + 48 + 56 + 30


def kernel(
    ids_ref, gates_ref, lat_ref, ctl_ref, og_ref, cs_ref, ng_ref, wi_ref, wo_ref,
    out_ref, sg_ref, gs_ref,
    zb, xst, xsl, rows, wi, wo, act, slope, fr, pb, own, part, codes, sel, gsel, pick, pick_t, meta, hid, gb,
    send, recv, lsem, free,
):
    me_s, me_e = lax.axis_index("seq"), lax.axis_index("expert")
    y, c = lax.div(me_s, 2), lax.rem(me_s, 2)
    z, x = lax.div(me_e, 4), lax.rem(me_e, 4)

    def z_at(delta):
        return (me_s, lax.rem(z + delta + 8, 8) * 4 + x)

    def x_at(delta):
        return (me_s, z * 4 + lax.rem(x + delta + 4, 4))

    odd = lax.rem(y, 2)
    sibling = (y * 2 + 1 - c, me_e)
    mates = {1: (lax.rem(y + 3 + 2 * odd, 4) * 2 + c, me_e), 2: ((y + 1 - 2 * odd) * 2 + c, me_e)}
    near = [
        (lax.rem(y + k // 4, 4) * 2 + c, z * 4 + lax.rem(x + k % 4, 4)) for k in range(1, 16)
    ]
    far = [
        (y * 2 + lax.rem(c + k % 2, 2), lax.rem(z + k // 2, 8) * 4 + x) for k in range(1, 16)
    ]
    peers = near + far

    barrier = pltpu.get_barrier_semaphore()
    for peer in peers:
        pl.semaphore_signal(barrier, inc=1, device_id=peer, device_id_type=MESH)

    local = []
    for k in range(2):
        local.append(
            pltpu.make_async_copy(
                wi_ref.at[0, :, pl.ds(256 * k, 256)], wi.at[:, pl.ds(SH * k, 256)], lsem.at[k]
            )
        )
        local.append(
            pltpu.make_async_copy(
                wo_ref.at[0, pl.ds(256 * k, 256)], wo.at[pl.ds(SH * k, 256)], lsem.at[2 + k]
            )
        )
    for copy in local:
        copy.start()

    scale, gain = cs_ref[...].reshape(1, D), ng_ref[...].reshape(1, D)
    hidden = lat_ref[...].astype(F32) + scale * ctl_ref[...].astype(F32)
    hid[...] = hidden
    inverse = 1.0 / jnp.sqrt(jnp.mean(hidden * hidden, axis=-1, keepdims=True) + 1e-06)
    zb[RES, 0:T] = (hidden * inverse * gain).astype(BF)
    zb[GRAD, 0:T] = og_ref[...]

    labels = iota((32, T), 0)
    hot0 = jnp.where(ids_ref[0:1] == labels, 1.0, 0.0)
    hot1 = jnp.where(ids_ref[1:2] == labels, 1.0, 0.0)
    before = jnp.where(iota((T, T), 0) < iota((T, T), 1), 1.0, 0.0).astype(BF)
    rank0 = jnp.sum(hot0 * nn(hot0.astype(BF), before), axis=0, keepdims=True)
    ahead = jnp.sum(hot0, axis=1, keepdims=True)
    rank1 = jnp.sum(hot1 * (nn(hot1.astype(BF), before) + ahead), axis=0, keepdims=True)
    line = iota((8, T), 0)
    mine = jnp.where(line == 0, ids_ref[0:1].astype(F32) * CAP + rank0, 0.0)
    mine = jnp.where(line == 1, ids_ref[1:2].astype(F32) * CAP + rank1, mine)
    mine = jnp.where(line == 2, gates_ref[0:1], mine)
    meta[0, 0:8] = jnp.where(line == 3, gates_ref[1:2], mine)

    pl.semaphore_wait(barrier, len(peers))
    wires = Wires(send, recv)

    def cols(q):
        return pl.ds(Q * q, Q)

    def z_own(u):
        a, q = u
        for h in range(2):
            for side in range(2):
                wires.start(
                    ("z", u, side, h),
                    zb.at[a, pl.ds(64 * h, 64), cols(q)],
                    zb.at[a, pl.ds(256 + T * side + 64 * h, 64), cols(q)],
                    z_at(1 - 2 * side),
                )

    def z_forward(u, d):
        a, q = u
        for h in range(2):
            for side in range(2):
                wires.arrived(("z", u, side, 2 * (d - 1) + h))
                src = zb.at[a, pl.ds(256 * d + T * side + 64 * h, 64), cols(q)]
                if d < 3:
                    dst = zb.at[a, pl.ds(256 * (d + 1) + T * side + 64 * h, 64), cols(q)]
                    wires.start(("z", u, side, 2 * d + h), src, dst, z_at(1 - 2 * side))
                elif side == h:
                    dst = zb.at[a, pl.ds(T + 64 * h, 64), cols(q)]
                    wires.start(("z", u, side, 6), src, dst, z_at(1 - 2 * side))

    def z_end(u):
        for side in range(2):
            wires.arrived(("z", u, side, 6))

    def z_left(u):
        for side in range(2):
            for m in range(7):
                wires.left(("z", u, side, m))

    def targets(g, k):
        return jnp.concatenate(
            [meta[0, pl.ds(16 * g + k, 1)], meta[0, pl.ds(16 * g + 8 + k, 1)]], axis=1
        )

    def prepare(g):
        first, second = codes[...] == targets(g, 0), codes[...] == targets(g, 1)
        sel[g] = jnp.where(first | second, 1.0, 0.0).astype(BF)

    def prepare_gates(g):
        first, second = codes[...] == targets(g, 0), codes[...] == targets(g, 1)
        gate = jnp.where(first, targets(g, 2), jnp.where(second, targets(g, 3), 0.0))
        high = gate.astype(BF)
        low = (gate - high.astype(F32)).astype(BF)
        eye = jnp.where(iota((192, 192), 0) == iota((192, 192), 1), 1.0, 0.0).astype(BF)
        gsel[g, 0] = tn(high, eye).astype(BF)
        gsel[g, 1] = tn(low, eye).astype(BF)

    def select(u, g):
        a, q = u
        got = nn(sel[g], zb[a, pl.ds(256 * g, 256), cols(q)]).astype(BF)
        xsl[a, pl.ds(PAIR * g, PAIR), cols(q)] = got[0:PAIR]
        xst[a, g, pl.ds(PAIR, 3 * PAIR), cols(q)] = got[PAIR:]
        for j in range(1, 4):
            wires.start(
                ("x", u, j, g),
                xst.at[a, g, pl.ds(PAIR * j, PAIR), cols(q)],
                xsl.at[a, pl.ds((4 * j + g) * PAIR, PAIR), cols(q)],
                x_at(j),
            )

    def block(o):
        return pl.ds(ROWS * o, ROWS)

    def compact(u):
        a, q = u
        for j in range(1, 4):
            for g in range(4):
                wires.left(("x", u, j, g))
            if q == 1:
                pl.semaphore_signal(free.at[a], inc=1, device_id=x_at(j), device_id_type=MESH)
        for g in (1, 2, 3, 0):
            for j in range(1, 4):
                wires.arrived(("x", u, j, g))
        rows[a, 0:ROWS, cols(q)] = nn(pick[...], xsl[a, :, cols(q)]).astype(BF)
        for k in (1, 2):
            wires.start(
                ("e", u, k), rows.at[a, block(0), cols(q)], rows.at[a, block(2 * k), cols(q)], mates[k]
            )
        wires.start(
            ("e", u, 0), rows.at[a, block(0), cols(q)], rows.at[a, block(1), cols(q)], sibling
        )

    def pass_rows(u):
        a, q = u
        for k in (1, 2):
            wires.arrived(("e", u, k))
            wires.start(
                ("e", u, 2 + k),
                rows.at[a, block(2 * k), cols(q)],
                rows.at[a, block(2 * k + 1), cols(q)],
                sibling,
            )

    def rows_here(a, k):
        for q in range(2):
            wires.arrived(("e", (a, q), 2 + k if k else 0))

    def forward(k):
        at, to, low, high = BLOCKS[k]
        rows_here(RES, k)

        @pl.loop(low // NT, high // NT)
        def _(i):
            tile = pl.ds(pl.multiple_of(i * NT, NT), NT)
            v = nn(rows[RES, pl.ds(at, 2 * ROWS)], wi[:, tile])
            inner = jnp.tanh(coeff * (v + cubic * v * v * v))
            act[pl.ds(to, 2 * ROWS), tile] = (0.5 * v * (1.0 + inner)).astype(BF)
            slope[pl.ds(to, 2 * ROWS), tile] = 0.5 * (1.0 + inner) + 0.5 * v * (
                1.0 - inner * inner
            ) * coeff * (1.0 + 3.0 * cubic * v * v)

    def backward(k):
        at, to, low, high = BLOCKS[k]
        rows_here(GRAD, k)

        @pl.loop(low // NT, high // NT)
        def _(i):
            tile = pl.ds(pl.multiple_of(i * NT, NT), NT)
            got = nt(rows[GRAD, pl.ds(at, 2 * ROWS)], wo[tile, :])
            act[pl.ds(to, 2 * ROWS), tile] = (got * slope[pl.ds(to, 2 * ROWS), tile]).astype(BF)

    def rows_left(a):
        for q in range(2):
            for k in range(5):
                wires.left(("e", (a, q), k))

    def result(q, k):
        at, to, low, high = BLOCKS[k]

        @pl.loop(0, Q // NT)
        def _(i):
            tile = pl.ds(pl.multiple_of(Q * q + i * NT, NT), NT)
            rows[RES, pl.ds(at, 2 * ROWS), tile] = nn(
                act[pl.ds(to, 2 * ROWS), low:high], wo[low:high, tile]
            ).astype(BF)

    def input_grad(q, k):
        at, to, low, high = BLOCKS[k]

        @pl.loop(0, Q // NT)
        def _(i):
            tile = pl.ds(pl.multiple_of(Q * q + i * NT, NT), NT)
            rows[GRAD, pl.ds(at, 2 * ROWS), tile] = nt(
                act[pl.ds(to, 2 * ROWS), low:high], wi[tile, low:high]
            ).astype(BF)

    def partial_sums(u, make):
        a, q = u
        for k in (1, 2, 0):
            make(q, k)
            wires.start(
                ("f", u, 2 + k if k else 0),
                rows.at[a, block(2 * k + 1), cols(q)],
                fr.at[a, 2 + k if k else 0, :, cols(q)],
                sibling,
            )

    def to_mates(u):
        a, q = u
        for k in (1, 2):
            wires.arrived(("f", u, 2 + k))
            rows[a, block(2 * k), cols(q)] = (
                rows[a, block(2 * k), cols(q)].astype(F32) + fr[a, 2 + k, :, cols(q)].astype(F32)
            ).astype(BF)
            wires.start(
                ("f", u, k), rows.at[a, block(2 * k), cols(q)], fr.at[a, k, :, cols(q)], mates[k]
            )

    def give_back(u):
        a, q = u
        for k in range(3):
            wires.arrived(("f", u, k))
        z_left(u)
        total = rows[a, block(0), cols(q)].astype(F32)
        for k in range(3):
            total = total + fr[a, k, :, cols(q)].astype(F32)
        zb[a, pl.ds(256, ROWS), cols(q)] = total.astype(BF)
        if q == 0:
            pl.semaphore_wait(free.at[a], 3)
        got = nn(pick_t[...], zb[a, pl.ds(256, ROWS), cols(q)]).astype(BF)
        for g in range(4):
            xst[a, g, 0:PAIR, cols(q)] = got[PAIR * g : PAIR * (g + 1)]
        xsl[a, pl.ds(4 * PAIR, 12 * PAIR), cols(q)] = got[4 * PAIR :]
        for g in (0, 3, 2, 1):
            for j in range(1, 4):
                wires.start(
                    ("r", u, j, g),
                    xsl.at[a, pl.ds((4 * j + g) * PAIR, PAIR), cols(q)],
                    xst.at[a, g, pl.ds(PAIR * j, PAIR), cols(q)],
                    x_at(-j),
                )

    def gathered(u, g):
        a, q = u
        for j in range(1, 4):
            wires.arrived(("r", u, j, g))
        got = xst[a, g, :, cols(q)]
        return nn(gsel[g, 0], got) + nn(gsel[g, 1], got)

    def z_back(u, side, m, src, g, h):
        a, q = u
        dst = pb.at[a, pl.ds(256 * g + T * side + 64 * h, 64), cols(q)]
        wires.start(("b", u, side, m), src, dst, z_at(2 * side - 1))

    def reduce_first(u):
        a, q = u
        got = gathered(u, 0)
        own[a, :, cols(q)] = got[0:T]
        zb[a, pl.ds(512, T), cols(q)] = got[T:].astype(BF)
        for side in range(2):
            z_back(u, side, 0, zb.at[a, pl.ds(512 + 64 * side, 64), cols(q)], 3, side)

    def reduce_next(u, g):
        a, q = u
        part[...] = gathered(u, g)
        order = ((0, 1), (1, 0), (0, 0), (1, 1)) if g == 3 else ((0, 0), (1, 0), (0, 1), (1, 1))
        for side, h in order:
            at = T * side + 64 * h
            value = part[at : at + 64]
            if g < 3 or side == h:
                wires.arrived(("b", u, side, 5 - 2 * g + h if g < 3 else 0))
                value = value + pb[a, pl.ds(256 * g + at, 64), cols(q)].astype(F32)
            pb[a, pl.ds(256 * g + at, 64), cols(q)] = value.astype(BF)
            src = pb.at[a, pl.ds(256 * g + at, 64), cols(q)]
            z_back(u, side, 7 - 2 * g + h, src, g - 1, h)

    def reduce_last(u):
        a, q = u
        for h in range(2):
            for side in range(2):
                wires.arrived(("b", u, side, 5 + h))
        return (
            own[a, :, cols(q)]
            + pb[a, 0:T, cols(q)].astype(F32)
            + pb[a, T:256, cols(q)].astype(F32)
        )

    r0, r1, g0, g1 = (RES, 0), (RES, 1), (GRAD, 0), (GRAD, 1)

    z_own(r0)
    for k in range(1, 8):
        wires.start(("mz", k), meta.at[0, pl.ds(0, 8)], meta.at[0, pl.ds(8 * Z_SLOT[k], 8)], z_at(k))
    for k, mate, to in ((0, 2, 256), (1, 1, 768)):
        wires.start(
            ("w", 0, k), wi_ref.at[0, :, pl.ds(256 * k, 256)], wi.at[:, pl.ds(to, 256)], mates[mate]
        )
    for k, mate, to in ((0, 2, 256), (1, 1, 768)):
        wires.start(
            ("w", 1, k), wo_ref.at[0, pl.ds(256 * k, 256)], wo.at[pl.ds(to, 256)], mates[mate]
        )
    spot = iota((PAIR, 256), 0)
    spot = jnp.where(spot >= CAP, spot - CAP + 1024, spot)
    spot = spot - jnp.where(iota((PAIR, 256), 1) >= T, 1024, 0)
    spot = jnp.where((spot >= 0) & (spot < CAP), spot, -65536).astype(F32)
    for j in range(4):
        first = (z * 4 + lax.rem(x + j, 4)) * CAP
        codes[pl.ds(PAIR * j, PAIR)] = spot + first.astype(F32)
    for k in range(1, 8):
        wires.arrived(("mz", k))
    for j in range(1, 4):
        wires.start(("mx", j), meta.at[0], meta.at[j], x_at(j))

    z_forward(r0, 1)
    z_own(r1)
    prepare(1)
    select(r0, 1)
    z_forward(r0, 2)
    prepare(2)
    select(r0, 2)
    z_forward(r1, 1)
    select(r1, 1)
    prepare(3)
    prepare(0)
    z_forward(r0, 3)
    select(r0, 3)

    for j in range(1, 4):
        wires.arrived(("mx", j))
    marks = meta[...].reshape(256, T)
    low = (me_e * CAP).astype(F32)
    named = (marks >= low) & (marks < low + CAP) & ((iota((256, T), 0) & 7) < 2)
    named = jnp.where(named, 1.0, 0.0).astype(BF)
    counts = nt(jnp.ones((8, T), BF), named).astype(BF)
    begin = (iota((256, N_SLOT), 0) >> 3) * CAP
    slot = iota((256, N_SLOT), 1)
    inside = (slot >= begin) & (slot < begin + CAP)
    filled = nn(counts, jnp.where(inside, 1.0, 0.0).astype(BF))
    offset = nn(counts, jnp.where(slot >= begin + CAP, 1.0, 0.0).astype(BF))
    slot = iota((8, N_SLOT), 1).astype(F32)
    rank = slot - CAP * jnp.floor((slot + 0.5) * (1.0 / CAP))
    place = jnp.where(rank < filled, offset + rank, -1.0)
    pick[...] = jnp.where(iota((ROWS, N_SLOT), 0).astype(F32) == place[0:1], 1.0, 0.0).astype(BF)

    z_forward(r1, 2)
    z_own(g0)
    select(r1, 2)
    z_end(r0)
    select(r0, 0)
    z_forward(r1, 3)
    select(r1, 3)
    compact(r0)
    z_forward(g0, 1)
    z_own(g1)
    select(g0, 1)
    z_end(r1)
    select(r1, 0)
    eye = jnp.where(iota((ROWS, ROWS), 0) == iota((ROWS, ROWS), 1), 1.0, 0.0).astype(BF)
    pick_t[...] = tn(pick[...], eye).astype(BF)
    prepare_gates(0)
    prepare_gates(1)
    z_forward(g0, 2)
    select(g0, 2)
    compact(r1)
    z_forward(g1, 1)
    select(g1, 1)
    for copy in local:
        copy.wait()
    for k in range(2):
        wires.arrived(("w", 0, k))
    forward(0)
    z_forward(g0, 3)
    select(g0, 3)
    prepare_gates(2)
    prepare_gates(3)
    z_forward(g1, 2)
    select(g1, 2)
    pass_rows(r0)
    z_end(g0)
    select(g0, 0)
    z_forward(g1, 3)
    select(g1, 3)
    compact(g0)
    pass_rows(r1)
    z_end(g1)
    select(g1, 0)
    forward(1)
    forward(2)
    for k in range(2):
        wires.arrived(("w", 1, k))
    rows_left(RES)
    partial_sums(r0, result)
    partial_sums(r1, result)
    to_mates(r0)
    compact(g1)
    to_mates(r1)
    pass_rows(g0)
    backward(0)
    give_back(r0)
    reduce_first(r0)
    pass_rows(g1)
    reduce_next(r0, 3)
    backward(1)
    backward(2)
    reduce_next(r0, 2)
    give_back(r1)
    rows_left(GRAD)
    partial_sums(g0, input_grad)
    reduce_next(r0, 1)
    to_mates(g0)
    partial_sums(g1, input_grad)
    reduce_first(r1)
    to_mates(g1)
    out_ref[:, cols(0)] = hid[:, cols(0)] + reduce_last(r0)
    reduce_next(r1, 3)
    reduce_next(r1, 2)
    give_back(g0)
    reduce_next(r1, 1)
    reduce_first(g0)
    give_back(g1)
    out_ref[:, cols(1)] = hid[:, cols(1)] + reduce_last(r1)
    reduce_next(g0, 3)
    reduce_first(g1)
    reduce_next(g0, 2)
    reduce_next(g1, 3)
    reduce_next(g0, 1)
    reduce_next(g1, 2)
    own[GRAD, :, cols(0)] = reduce_last(g0)
    reduce_next(g1, 1)
    own[GRAD, :, cols(1)] = reduce_last(g1)

    hidden = hid[...]
    inverse = 1.0 / jnp.sqrt(jnp.mean(hidden * hidden, axis=-1, keepdims=True) + 1e-06)
    normed = hidden * inverse
    normed_grad = own[GRAD] * gain
    mean = jnp.mean(normed_grad * normed, axis=-1, keepdims=True)
    sum_grad = inverse * (normed_grad - normed * mean) + og_ref[...].astype(F32)
    sg_ref[...] = sum_grad

    total = jnp.sum(sum_grad * ctl_ref[...].astype(F32), axis=0, keepdims=True)
    for base, here, others in ((0, y * 4 + x, near), (16, z * 2 + c, far)):
        gb[base + here] = total
        for k, other in enumerate(others):
            wires.start(("g", base, k), gb.at[base + here], gb.at[base + here], other)
        for k in range(len(others)):
            wires.arrived(("g", base, k))
        total = gb[base]
        for k in range(1, 16):
            total = total + gb[base + k]
    gs_ref[...] = total.reshape(D)
    wires.finish()


def body(
    latents, control, control_scale, norm_gain, expert_ids, gate_weights, expert_in, expert_out, out_grad
):
    vmem = pl.BlockSpec(memory_space=pltpu.VMEM)
    hbm = pl.BlockSpec(memory_space=pl.ANY)
    output, sum_grad, grad_scale = pl.pallas_call(
        kernel,
        out_shape=(
            jax.ShapeDtypeStruct((T, D), F32),
            jax.ShapeDtypeStruct((T, D), F32),
            jax.ShapeDtypeStruct((D,), F32),
        ),
        in_specs=[vmem] * 7 + [hbm] * 2,
        out_specs=(vmem,) * 3,
        scratch_shapes=[
            pltpu.VMEM((2, 4 * 256, D), BF),
            pltpu.VMEM((2, 4, 4 * PAIR, D), BF),
            pltpu.VMEM((2, N_SLOT, D), BF),
            pltpu.VMEM((2, 6 * ROWS, D), BF),
            pltpu.VMEM((D, HID), BF),
            pltpu.VMEM((HID, D), BF),
            pltpu.VMEM((4 * ROWS, HID), BF),
            pltpu.VMEM((4 * ROWS, HID), F32),
            pltpu.VMEM((2, 5, ROWS, D), BF),
            pltpu.VMEM((2, 4 * 256, D), BF),
            pltpu.VMEM((2, T, D), F32),
            pltpu.VMEM((256, Q), F32),
            pltpu.VMEM((4 * PAIR, 256), F32),
            pltpu.VMEM((4, 4 * PAIR, 256), BF),
            pltpu.VMEM((4, 2, 256, 4 * PAIR), BF),
            pltpu.VMEM((ROWS, N_SLOT), BF),
            pltpu.VMEM((N_SLOT, ROWS), BF),
            pltpu.VMEM((4, 64, T), F32),
            pltpu.VMEM((T, D), F32),
            pltpu.VMEM((32, 1, D), F32),
            pltpu.SemaphoreType.DMA((N_COPIES,)),
            pltpu.SemaphoreType.DMA((N_COPIES,)),
            pltpu.SemaphoreType.DMA((4,)),
            pltpu.SemaphoreType.REGULAR((2,)),
        ],
        compiler_params=pltpu.CompilerParams(
            collective_id=0, has_side_effects=True, vmem_limit_bytes=63 * 1024 * 1024
        ),
    )(
        expert_ids.T, gate_weights.T, latents, control, out_grad, control_scale, norm_gain,
        expert_in, expert_out,
    )
    return output.astype(BF), sum_grad.astype(BF), (sum_grad * control_scale).astype(BF), grad_scale


def solution(mesh):
    return jax.shard_map(
        body,
        mesh=mesh,
        in_specs=(
            P(("seq", "expert"), None),
            P(("seq", "expert"), None),
            P(),
            P(),
            P(("seq", "expert"), None),
            P(("seq", "expert"), None),
            P("expert", None, "seq"),
            P("expert", "seq", None),
            P(("seq", "expert"), None),
        ),
        out_specs=(
            P(("seq", "expert"), None),
            P(("seq", "expert"), None),
            P(("seq", "expert"), None),
            P(),
        ),
        check_vma=False,
    )
```

```python
import jax
import jax.numpy as jnp
from jax import lax
from jax.experimental import pallas as pl
from jax.experimental.pallas import tpu as pltpu
from jax.sharding import PartitionSpec as P

coeff = 0.7978845608
cubic = 0.044715

MESH = pl.DeviceIdType.MESH
BF = jnp.bfloat16
F32 = jnp.float32

T = 128
CAP = 24
PAIR = 2 * CAP
ROWS = 256
D = 1536
SH = 512
HID = 2 * SH
RES, GRAD = 0, 1
NT = 256
Q = D // 2
N_SLOT = 32 * CAP
Z_SLOT = {1: 2, 2: 4, 3: 6, 4: 1, 5: 7, 6: 5, 7: 3}


def nn(a, b):
    return lax.dot_general(a, b, (((1,), (0,)), ((), ())), preferred_element_type=F32)


def nt(a, b):
    return lax.dot_general(a, b, (((1,), (1,)), ((), ())), preferred_element_type=F32)


def tn(a, b):
    return lax.dot_general(a, b, (((0,), (0,)), ((), ())), preferred_element_type=F32)


def iota(shape, dim):
    return lax.broadcasted_iota(jnp.int32, shape, dim)


class Wires:
    def __init__(self, send, recv):
        self.send, self.recv = send, recv
        self.copies = {}
        self.sent = set()

    def start(self, key, src, dst, device):
        place = len(self.copies)
        copy = pltpu.make_async_remote_copy(
            src_ref=src,
            dst_ref=dst,
            send_sem=self.send.at[place],
            recv_sem=self.recv.at[place],
            device_id=device,
            device_id_type=MESH,
        )
        copy.start()
        self.copies[key] = copy

    def arrived(self, key):
        self.copies[key].wait_recv()

    def left(self, key):
        if key not in self.sent:
            self.sent.add(key)
            self.copies[key].wait_send()

    def finish(self):
        for key in self.copies:
            self.left(key)


N_COPIES = 56 + 7 + 3 + 3 + 48 + 12 + 12 + 48 + 56 + 30


def kernel(
    ids_ref, gates_ref, lat_ref, ctl_ref, og_ref, cs_ref, ng_ref, wi_ref, wo_ref,
    out_ref, sg_ref, gs_ref,
    zb, xst, xsl, rows, wi, wo, act, slope, fr, pb, own, part, codes, sel, gsel, pick, pick_t, meta, hid, inv, lat, ctl, gb,
    send, recv, lsem, free,
):
    me_s, me_e = lax.axis_index("seq"), lax.axis_index("expert")
    y, c = lax.div(me_s, 2), lax.rem(me_s, 2)
    z, x = lax.div(me_e, 4), lax.rem(me_e, 4)

    def z_at(delta):
        return (me_s, lax.rem(z + delta + 8, 8) * 4 + x)

    def x_at(delta):
        return (me_s, z * 4 + lax.rem(x + delta + 4, 4))

    odd = lax.rem(y, 2)
    sibling = (y * 2 + 1 - c, me_e)
    row_mate = (lax.rem(y + 3 + 2 * odd, 4) * 2 + c, me_e)
    weight_mate = ((y + 1 - 2 * odd) * 2 + c, me_e)
    near = [
        (lax.rem(y + k // 4, 4) * 2 + c, z * 4 + lax.rem(x + k % 4, 4)) for k in range(1, 16)
    ]
    far = [
        (y * 2 + lax.rem(c + k % 2, 2), lax.rem(z + k // 2, 8) * 4 + x) for k in range(1, 16)
    ]
    peers = near + far

    barrier = pltpu.get_barrier_semaphore()
    for peer in peers:
        pl.semaphore_signal(barrier, inc=1, device_id=peer, device_id_type=MESH)

    tokens = [
        pltpu.make_async_copy(lat_ref, lat, lsem.at[2]),
        pltpu.make_async_copy(ctl_ref, ctl, lsem.at[3]),
        pltpu.make_async_copy(og_ref, zb.at[GRAD, pl.ds(0, T)], lsem.at[4]),
    ]
    local = [
        pltpu.make_async_copy(wi_ref.at[0], wi.at[:, pl.ds(0, SH)], lsem.at[0]),
        pltpu.make_async_copy(wo_ref.at[0], wo.at[pl.ds(0, SH)], lsem.at[1]),
    ]
    for copy in tokens + local:
        copy.start()

    scale, gain = cs_ref[...].reshape(1, D), ng_ref[...].reshape(1, D)
    for load in tokens:
        load.wait()
    hidden = lat[...].astype(F32) + scale * ctl[...].astype(F32)
    hid[...] = hidden
    inverse = 1.0 / jnp.sqrt(jnp.mean(hidden * hidden, axis=-1, keepdims=True) + 1e-06)
    zb[RES, 0:T] = (hidden * inverse * gain).astype(BF)
    inv[...] = inverse

    labels = iota((32, T), 0)
    hot0 = jnp.where(ids_ref[0:1] == labels, 1.0, 0.0)
    hot1 = jnp.where(ids_ref[1:2] == labels, 1.0, 0.0)
    before = jnp.where(iota((T, T), 0) < iota((T, T), 1), 1.0, 0.0).astype(BF)
    rank0 = jnp.sum(hot0 * nn(hot0.astype(BF), before), axis=0, keepdims=True)
    ahead = jnp.sum(hot0, axis=1, keepdims=True)
    rank1 = jnp.sum(hot1 * (nn(hot1.astype(BF), before) + ahead), axis=0, keepdims=True)
    line = iota((8, T), 0)
    mine = jnp.where(line == 0, ids_ref[0:1].astype(F32) * CAP + rank0, 0.0)
    mine = jnp.where(line == 1, ids_ref[1:2].astype(F32) * CAP + rank1, mine)
    mine = jnp.where(line == 2, gates_ref[0:1], mine)
    meta[0, 0:8] = jnp.where(line == 3, gates_ref[1:2], mine)

    pl.semaphore_wait(barrier, len(peers))
    wires = Wires(send, recv)

    def cols(q):
        return pl.ds(Q * q, Q)

    def z_own(u):
        a, q = u
        for h in range(2):
            for side in range(2):
                wires.start(
                    ("z", u, side, h),
                    zb.at[a, pl.ds(64 * h, 64), cols(q)],
                    zb.at[a, pl.ds(256 + T * side + 64 * h, 64), cols(q)],
                    z_at(1 - 2 * side),
                )

    def z_forward(u, d):
        a, q = u
        for h in range(2):
            for side in range(2):
                wires.arrived(("z", u, side, 2 * (d - 1) + h))
                src = zb.at[a, pl.ds(256 * d + T * side + 64 * h, 64), cols(q)]
                if d < 3:
                    dst = zb.at[a, pl.ds(256 * (d + 1) + T * side + 64 * h, 64), cols(q)]
                    wires.start(("z", u, side, 2 * d + h), src, dst, z_at(1 - 2 * side))
                elif side == h:
                    dst = zb.at[a, pl.ds(T + 64 * h, 64), cols(q)]
                    wires.start(("z", u, side, 6), src, dst, z_at(1 - 2 * side))

    def z_end(u):
        for side in range(2):
            wires.arrived(("z", u, side, 6))

    def z_left(u):
        for side in range(2):
            for m in range(7):
                wires.left(("z", u, side, m))

    def targets(g, k):
        return jnp.concatenate(
            [meta[0, pl.ds(16 * g + k, 1)], meta[0, pl.ds(16 * g + 8 + k, 1)]], axis=1
        )

    def prepare(g):
        first, second = codes[...] == targets(g, 0), codes[...] == targets(g, 1)
        sel[g] = jnp.where(first | second, 1.0, 0.0).astype(BF)

    def prepare_gates(g):
        first, second = codes[...] == targets(g, 0), codes[...] == targets(g, 1)
        gate = jnp.where(first, targets(g, 2), jnp.where(second, targets(g, 3), 0.0))
        high = gate.astype(BF)
        low = (gate - high.astype(F32)).astype(BF)
        eye = jnp.where(iota((192, 192), 0) == iota((192, 192), 1), 1.0, 0.0).astype(BF)
        gsel[g, 0] = tn(high, eye).astype(BF)
        gsel[g, 1] = tn(low, eye).astype(BF)

    def select(u, g):
        a, q = u
        got = nn(sel[g], zb[a, pl.ds(256 * g, 256), cols(q)]).astype(BF)
        xsl[a, pl.ds(PAIR * g, PAIR), cols(q)] = got[0:PAIR]
        xst[a, g, pl.ds(PAIR, 3 * PAIR), cols(q)] = got[PAIR:]
        for j in range(1, 4):
            wires.start(
                ("x", u, j, g),
                xst.at[a, g, pl.ds(PAIR * j, PAIR), cols(q)],
                xsl.at[a, pl.ds((4 * j + g) * PAIR, PAIR), cols(q)],
                x_at(j),
            )

    def block(o):
        return pl.ds(ROWS * o, ROWS)

    def compact(u):
        a, q = u
        for j in range(1, 4):
            for g in range(4):
                wires.left(("x", u, j, g))
            if q == 1:
                pl.semaphore_signal(free.at[a], inc=1, device_id=x_at(j), device_id_type=MESH)
        for g in (1, 2, 3, 0):
            for j in range(1, 4):
                wires.arrived(("x", u, j, g))
        rows[a, 0:ROWS, cols(q)] = nn(pick[...], xsl[a, :, cols(q)]).astype(BF)
        wires.start(
            ("e", u, 0), rows.at[a, block(0), cols(q)], rows.at[a, block(1), cols(q)], sibling
        )

    def rows_to_mate(u):
        a, q = u
        wires.start(
            ("e", u, 1), rows.at[a, block(0), cols(q)], rows.at[a, block(2), cols(q)], row_mate
        )

    def pass_rows(u):
        a, q = u
        wires.arrived(("e", u, 1))
        wires.start(
            ("e", u, 2), rows.at[a, block(2), cols(q)], rows.at[a, block(3), cols(q)], sibling
        )

    def rows_here(a, k):
        for q in range(2):
            wires.arrived(("e", (a, q), 2 * k))

    def forward(k):
        here = pl.ds(2 * ROWS * k, 2 * ROWS)
        rows_here(RES, k)

        @pl.loop(0, HID // NT)
        def _(i):
            tile = pl.ds(pl.multiple_of(i * NT, NT), NT)
            v = nn(rows[RES, here], wi[:, tile])
            inner = jnp.tanh(coeff * (v + cubic * v * v * v))
            act[here, tile] = (0.5 * v * (1.0 + inner)).astype(BF)
            slope[here, tile] = 0.5 * (1.0 + inner) + 0.5 * v * (
                1.0 - inner * inner
            ) * coeff * (1.0 + 3.0 * cubic * v * v)

    def backward(k):
        here = pl.ds(2 * ROWS * k, 2 * ROWS)
        rows_here(GRAD, k)

        @pl.loop(0, HID // NT)
        def _(i):
            tile = pl.ds(pl.multiple_of(i * NT, NT), NT)
            got = nt(rows[GRAD, here], wo[tile, :])
            act[here, tile] = (got * slope[here, tile]).astype(BF)

    def rows_left(a):
        for q in range(2):
            for k in range(3):
                wires.left(("e", (a, q), k))

    def result(q, k):
        here = pl.ds(2 * ROWS * k, 2 * ROWS)

        @pl.loop(0, Q // NT)
        def _(i):
            tile = pl.ds(pl.multiple_of(Q * q + i * NT, NT), NT)
            rows[RES, here, tile] = nn(
                act[here, :], wo[:, tile]
            ).astype(BF)

    def input_grad(q, k):
        here = pl.ds(2 * ROWS * k, 2 * ROWS)

        @pl.loop(0, Q // NT)
        def _(i):
            tile = pl.ds(pl.multiple_of(Q * q + i * NT, NT), NT)
            rows[GRAD, here, tile] = nt(
                act[here, :], wi[tile, :]
            ).astype(BF)

    def partial_sums(u, make):
        a, q = u
        for k in (1, 0):
            make(q, k)
            wires.start(
                ("f", u, 2 * k),
                rows.at[a, block(2 * k + 1), cols(q)],
                fr.at[a, 2 * k, :, cols(q)],
                sibling,
            )

    def to_mate(u):
        a, q = u
        wires.arrived(("f", u, 2))
        rows[a, block(2), cols(q)] = (
            rows[a, block(2), cols(q)].astype(F32) + fr[a, 2, :, cols(q)].astype(F32)
        ).astype(BF)
        wires.start(("f", u, 1), rows.at[a, block(2), cols(q)], fr.at[a, 1, :, cols(q)], row_mate)

    def give_back(u):
        a, q = u
        for k in range(2):
            wires.arrived(("f", u, k))
        z_left(u)
        total = rows[a, block(0), cols(q)].astype(F32)
        for k in range(2):
            total = total + fr[a, k, :, cols(q)].astype(F32)
        zb[a, pl.ds(256, ROWS), cols(q)] = total.astype(BF)
        if q == 0:
            pl.semaphore_wait(free.at[a], 3)
        got = nn(pick_t[...], zb[a, pl.ds(256, ROWS), cols(q)]).astype(BF)
        for g in range(4):
            xst[a, g, 0:PAIR, cols(q)] = got[PAIR * g : PAIR * (g + 1)]
        xsl[a, pl.ds(4 * PAIR, 12 * PAIR), cols(q)] = got[4 * PAIR :]
        slots_back(u, 0)
        slots_back(u, 3)

    def slots_back(u, g):
        a, q = u
        for j in range(1, 4):
            wires.start(
                ("r", u, j, g),
                xsl.at[a, pl.ds((4 * j + g) * PAIR, PAIR), cols(q)],
                xst.at[a, g, pl.ds(PAIR * j, PAIR), cols(q)],
                x_at(-j),
            )

    def gathered(u, g):
        a, q = u
        for j in range(1, 4):
            wires.arrived(("r", u, j, g))
        got = xst[a, g, :, cols(q)]
        return nn(gsel[g, 0], got) + nn(gsel[g, 1], got)

    def z_back(u, side, m, src, g, h):
        a, q = u
        dst = pb.at[a, pl.ds(256 * g + T * side + 64 * h, 64), cols(q)]
        wires.start(("b", u, side, m), src, dst, z_at(2 * side - 1))

    def reduce_first(u):
        a, q = u
        got = gathered(u, 0)
        slots_back(u, 2)
        slots_back(u, 1)
        own[a, :, cols(q)] = got[0:T]
        zb[a, pl.ds(512, T), cols(q)] = got[T:].astype(BF)
        for side in range(2):
            z_back(u, side, 0, zb.at[a, pl.ds(512 + 64 * side, 64), cols(q)], 3, side)

    def reduce_next(u, g):
        a, q = u
        part[...] = gathered(u, g)
        order = ((0, 1), (1, 0), (0, 0), (1, 1)) if g == 3 else ((0, 0), (1, 0), (0, 1), (1, 1))
        for side, h in order:
            at = T * side + 64 * h
            value = part[at : at + 64]
            if g < 3 or side == h:
                wires.arrived(("b", u, side, 5 - 2 * g + h if g < 3 else 0))
                value = value + pb[a, pl.ds(256 * g + at, 64), cols(q)].astype(F32)
            pb[a, pl.ds(256 * g + at, 64), cols(q)] = value.astype(BF)
            src = pb.at[a, pl.ds(256 * g + at, 64), cols(q)]
            z_back(u, side, 7 - 2 * g + h, src, g - 1, h)

    def reduce_last(u):
        a, q = u
        for h in range(2):
            for side in range(2):
                wires.arrived(("b", u, side, 5 + h))
        return (
            own[a, :, cols(q)]
            + pb[a, 0:T, cols(q)].astype(F32)
            + pb[a, T:256, cols(q)].astype(F32)
        )

    r0, r1, g0, g1 = (RES, 0), (RES, 1), (GRAD, 0), (GRAD, 1)

    z_own(r0)
    for k in range(1, 8):
        wires.start(("mz", k), meta.at[0, pl.ds(0, 8)], meta.at[0, pl.ds(8 * Z_SLOT[k], 8)], z_at(k))
    wires.start(("w", 0), wi_ref.at[0], wi.at[:, pl.ds(SH, SH)], weight_mate)

    def more_weights(q):
        wires.start(
            ("w", 1 + q), wo_ref.at[0, :, cols(q)], wo.at[pl.ds(SH, SH), cols(q)], weight_mate
        )

    spot = iota((PAIR, 256), 0)
    spot = jnp.where(spot >= CAP, spot - CAP + 1024, spot)
    spot = spot - jnp.where(iota((PAIR, 256), 1) >= T, 1024, 0)
    spot = jnp.where((spot >= 0) & (spot < CAP), spot, -65536).astype(F32)
    for j in range(4):
        first = (z * 4 + lax.rem(x + j, 4)) * CAP
        codes[pl.ds(PAIR * j, PAIR)] = spot + first.astype(F32)
    for k in range(1, 8):
        wires.arrived(("mz", k))
    for j in range(1, 4):
        wires.start(("mx", j), meta.at[0], meta.at[j], x_at(j))

    z_forward(r0, 1)
    z_own(r1)
    prepare(1)
    select(r0, 1)
    z_forward(r0, 2)
    prepare(2)
    select(r0, 2)
    z_forward(r1, 1)
    select(r1, 1)
    prepare(3)
    prepare(0)
    z_forward(r0, 3)
    select(r0, 3)

    for j in range(1, 4):
        wires.arrived(("mx", j))
    marks = meta[...].reshape(256, T)
    low = (me_e * CAP).astype(F32)
    named = (marks >= low) & (marks < low + CAP) & ((iota((256, T), 0) & 7) < 2)
    named = jnp.where(named, 1.0, 0.0).astype(BF)
    counts = nt(jnp.ones((8, T), BF), named).astype(BF)
    begin = (iota((256, N_SLOT), 0) >> 3) * CAP
    slot = iota((256, N_SLOT), 1)
    inside = (slot >= begin) & (slot < begin + CAP)
    filled = nn(counts, jnp.where(inside, 1.0, 0.0).astype(BF))
    offset = nn(counts, jnp.where(slot >= begin + CAP, 1.0, 0.0).astype(BF))
    slot = iota((8, N_SLOT), 1).astype(F32)
    rank = slot - CAP * jnp.floor((slot + 0.5) * (1.0 / CAP))
    place = jnp.where(rank < filled, offset + rank, -1.0)
    pick[...] = jnp.where(iota((ROWS, N_SLOT), 0).astype(F32) == place[0:1], 1.0, 0.0).astype(BF)

    z_forward(r1, 2)
    z_own(g0)
    select(r1, 2)
    z_end(r0)
    select(r0, 0)
    z_forward(r1, 3)
    select(r1, 3)
    more_weights(0)
    compact(r0)
    rows_to_mate(r0)
    z_forward(g0, 1)
    z_own(g1)
    select(g0, 1)
    z_end(r1)
    select(r1, 0)
    eye = jnp.where(iota((ROWS, ROWS), 0) == iota((ROWS, ROWS), 1), 1.0, 0.0).astype(BF)
    pick_t[...] = tn(pick[...], eye).astype(BF)
    prepare_gates(0)
    prepare_gates(1)
    z_forward(g0, 2)
    select(g0, 2)
    compact(r1)
    rows_to_mate(r1)
    z_forward(g1, 1)
    select(g1, 1)
    pass_rows(r0)
    for copy in local:
        copy.wait()
    wires.arrived(("w", 0))
    forward(0)
    z_forward(g0, 3)
    select(g0, 3)
    more_weights(1)
    prepare_gates(2)
    prepare_gates(3)
    z_forward(g1, 2)
    select(g1, 2)
    pass_rows(r1)
    z_end(g0)
    select(g0, 0)
    forward(1)
    wires.arrived(("w", 1))
    rows_left(RES)
    partial_sums(r0, result)
    z_forward(g1, 3)
    select(g1, 3)
    to_mate(r0)
    compact(g0)
    rows_to_mate(g0)
    z_end(g1)
    select(g1, 0)
    wires.arrived(("w", 2))
    partial_sums(r1, result)
    compact(g1)
    rows_to_mate(g1)
    give_back(r0)
    to_mate(r1)
    pass_rows(g0)
    backward(0)
    reduce_first(r0)
    reduce_next(r0, 3)
    pass_rows(g1)
    backward(1)
    rows_left(GRAD)
    partial_sums(g0, input_grad)
    give_back(r1)
    reduce_next(r0, 2)
    to_mate(g0)
    partial_sums(g1, input_grad)
    reduce_next(r0, 1)
    reduce_first(r1)
    to_mate(g1)
    out_ref[:, cols(0)] = hid[:, cols(0)] + reduce_last(r0)
    reduce_next(r1, 3)
    give_back(g0)
    reduce_next(r1, 2)
    reduce_next(r1, 1)
    reduce_first(g0)
    give_back(g1)
    reduce_next(g0, 3)
    out_ref[:, cols(1)] = hid[:, cols(1)] + reduce_last(r1)
    reduce_first(g1)
    reduce_next(g0, 2)
    reduce_next(g1, 3)
    reduce_next(g0, 1)
    reduce_next(g1, 2)
    own[GRAD, :, cols(0)] = reduce_last(g0)
    reduce_next(g1, 1)
    own[GRAD, :, cols(1)] = reduce_last(g1)

    inverse = inv[...]
    normed = hid[...] * inverse
    normed_grad = own[GRAD] * gain
    mean = jnp.mean(normed_grad * normed, axis=-1, keepdims=True)
    sum_grad = inverse * (normed_grad - normed * mean) + zb[GRAD, 0:T].astype(F32)
    sg_ref[...] = sum_grad

    total = jnp.sum(sum_grad * ctl[...].astype(F32), axis=0, keepdims=True)
    for base, here, others in ((0, y * 4 + x, near), (16, z * 2 + c, far)):
        gb[base + here] = total
        for k, other in enumerate(others):
            wires.start(("g", base, k), gb.at[base + here], gb.at[base + here], other)
        for k in range(len(others)):
            wires.arrived(("g", base, k))
        total = gb[base]
        for k in range(1, 16):
            total = total + gb[base + k]
    gs_ref[...] = total.reshape(D)
    wires.finish()


def body(
    latents, control, control_scale, norm_gain, expert_ids, gate_weights, expert_in, expert_out, out_grad
):
    vmem = pl.BlockSpec(memory_space=pltpu.VMEM)
    hbm = pl.BlockSpec(memory_space=pl.ANY)
    output, sum_grad, grad_scale = pl.pallas_call(
        kernel,
        out_shape=(
            jax.ShapeDtypeStruct((T, D), F32),
            jax.ShapeDtypeStruct((T, D), F32),
            jax.ShapeDtypeStruct((D,), F32),
        ),
        in_specs=[vmem] * 2 + [hbm] * 3 + [vmem] * 2 + [hbm] * 2,
        out_specs=(vmem,) * 3,
        scratch_shapes=[
            pltpu.VMEM((2, 4 * 256, D), BF),
            pltpu.VMEM((2, 4, 4 * PAIR, D), BF),
            pltpu.VMEM((2, N_SLOT, D), BF),
            pltpu.VMEM((2, 4 * ROWS, D), BF),
            pltpu.VMEM((D, HID), BF),
            pltpu.VMEM((HID, D), BF),
            pltpu.VMEM((4 * ROWS, HID), BF),
            pltpu.VMEM((4 * ROWS, HID), F32),
            pltpu.VMEM((2, 3, ROWS, D), BF),
            pltpu.VMEM((2, 4 * 256, D), BF),
            pltpu.VMEM((2, T, D), F32),
            pltpu.VMEM((256, Q), F32),
            pltpu.VMEM((4 * PAIR, 256), F32),
            pltpu.VMEM((4, 4 * PAIR, 256), BF),
            pltpu.VMEM((4, 2, 256, 4 * PAIR), BF),
            pltpu.VMEM((ROWS, N_SLOT), BF),
            pltpu.VMEM((N_SLOT, ROWS), BF),
            pltpu.VMEM((4, 64, T), F32),
            pltpu.VMEM((T, D), F32),
            pltpu.VMEM((T, 1), F32),
            pltpu.VMEM((T, D), BF),
            pltpu.VMEM((T, D), BF),
            pltpu.VMEM((32, 1, D), F32),
            pltpu.SemaphoreType.DMA((N_COPIES,)),
            pltpu.SemaphoreType.DMA((N_COPIES,)),
            pltpu.SemaphoreType.DMA((5,)),
            pltpu.SemaphoreType.REGULAR((2,)),
        ],
        compiler_params=pltpu.CompilerParams(
            collective_id=0, has_side_effects=True, vmem_limit_bytes=63 * 1024 * 1024
        ),
    )(
        expert_ids.T, gate_weights.T, latents, control, out_grad, control_scale, norm_gain,
        expert_in, expert_out,
    )
    return output.astype(BF), sum_grad.astype(BF), (sum_grad * control_scale).astype(BF), grad_scale


def solution(mesh):
    return jax.shard_map(
        body,
        mesh=mesh,
        in_specs=(
            P(("seq", "expert"), None),
            P(("seq", "expert"), None),
            P(),
            P(),
            P(("seq", "expert"), None),
            P(("seq", "expert"), None),
            P("expert", None, "seq"),
            P("expert", "seq", None),
            P(("seq", "expert"), None),
        ),
        out_specs=(
            P(("seq", "expert"), None),
            P(("seq", "expert"), None),
            P(("seq", "expert"), None),
            P(),
        ),
        check_vma=False,
    )
```

```python
import jax
import jax.numpy as jnp
from jax import lax
from jax.experimental import pallas as pl
from jax.experimental.pallas import tpu as pltpu
from jax.sharding import PartitionSpec as P

coeff = 0.7978845608
cubic = 0.044715

MESH = pl.DeviceIdType.MESH
BF = jnp.bfloat16
F32 = jnp.float32

T = 128
CAP = 24
PAIR = 2 * CAP
ROWS = 256
D = 1536
SH = 512
HID = 2 * SH
RES, GRAD = 0, 1
NT = 256
Q = D // 2
N_SLOT = 32 * CAP
Z_SLOT = {1: 2, 2: 4, 3: 6, 4: 1, 5: 7, 6: 5, 7: 3}


def nn(a, b):
    return lax.dot_general(a, b, (((1,), (0,)), ((), ())), preferred_element_type=F32)


def nt(a, b):
    return lax.dot_general(a, b, (((1,), (1,)), ((), ())), preferred_element_type=F32)


def tn(a, b):
    return lax.dot_general(a, b, (((0,), (0,)), ((), ())), preferred_element_type=F32)


def iota(shape, dim):
    return lax.broadcasted_iota(jnp.int32, shape, dim)


class Wires:
    def __init__(self, send, recv):
        self.send, self.recv = send, recv
        self.copies = {}
        self.sent = set()

    def start(self, key, src, dst, device):
        place = len(self.copies)
        copy = pltpu.make_async_remote_copy(
            src_ref=src,
            dst_ref=dst,
            send_sem=self.send.at[place],
            recv_sem=self.recv.at[place],
            device_id=device,
            device_id_type=MESH,
        )
        copy.start()
        self.copies[key] = copy

    def arrived(self, key):
        self.copies[key].wait_recv()

    def left(self, key):
        if key not in self.sent:
            self.sent.add(key)
            self.copies[key].wait_send()

    def finish(self):
        for key in self.copies:
            self.left(key)


N_COPIES = 56 + 7 + 3 + 3 + 48 + 12 + 12 + 48 + 56 + 30


def kernel(
    ids_ref, gates_ref, lat_ref, ctl_ref, og_ref, cs_ref, ng_ref, wi_ref, wo_ref,
    out_ref, sg_ref, gs_ref,
    zb, xst, xsl, rows, wi, wo, act, slope, fr, pb, own, part, codes, sel, gsel, pick, pick_t, meta, hid, inv, lat, ctl, gb,
    send, recv, lsem, free,
):
    me_s, me_e = lax.axis_index("seq"), lax.axis_index("expert")
    y, c = lax.div(me_s, 2), lax.rem(me_s, 2)
    z, x = lax.div(me_e, 4), lax.rem(me_e, 4)

    def z_at(delta):
        return (me_s, lax.rem(z + delta + 8, 8) * 4 + x)

    def x_at(delta):
        return (me_s, z * 4 + lax.rem(x + delta + 4, 4))

    odd = lax.rem(y, 2)
    sibling = (y * 2 + 1 - c, me_e)
    row_mate = (lax.rem(y + 3 + 2 * odd, 4) * 2 + c, me_e)
    weight_mate = ((y + 1 - 2 * odd) * 2 + c, me_e)
    near = [
        (lax.rem(y + k // 4, 4) * 2 + c, z * 4 + lax.rem(x + k % 4, 4)) for k in range(1, 16)
    ]
    far = [
        (y * 2 + lax.rem(c + k % 2, 2), lax.rem(z + k // 2, 8) * 4 + x) for k in range(1, 16)
    ]
    peers = near + far

    barrier = pltpu.get_barrier_semaphore()
    for peer in peers:
        pl.semaphore_signal(barrier, inc=1, device_id=peer, device_id_type=MESH)

    tokens = [
        pltpu.make_async_copy(lat_ref, lat, lsem.at[2]),
        pltpu.make_async_copy(ctl_ref, ctl, lsem.at[3]),
        pltpu.make_async_copy(og_ref, zb.at[GRAD, pl.ds(0, T)], lsem.at[4]),
    ]
    local = [
        pltpu.make_async_copy(wi_ref.at[0], wi.at[:, pl.ds(0, SH)], lsem.at[0]),
        pltpu.make_async_copy(wo_ref.at[0], wo.at[pl.ds(0, SH)], lsem.at[1]),
    ]
    for copy in tokens + local:
        copy.start()

    scale, gain = cs_ref[...].reshape(1, D), ng_ref[...].reshape(1, D)
    for load in tokens:
        load.wait()
    hidden = lat[...].astype(F32) + scale * ctl[...].astype(F32)
    hid[...] = hidden
    inverse = 1.0 / jnp.sqrt(jnp.mean(hidden * hidden, axis=-1, keepdims=True) + 1e-06)
    zb[RES, 0:T] = (hidden * inverse * gain).astype(BF)
    inv[...] = inverse

    labels = iota((32, T), 0)
    hot0 = jnp.where(ids_ref[0:1] == labels, 1.0, 0.0)
    hot1 = jnp.where(ids_ref[1:2] == labels, 1.0, 0.0)
    before = jnp.where(iota((T, T), 0) < iota((T, T), 1), 1.0, 0.0).astype(BF)
    rank0 = jnp.sum(hot0 * nn(hot0.astype(BF), before), axis=0, keepdims=True)
    ahead = jnp.sum(hot0, axis=1, keepdims=True)
    rank1 = jnp.sum(hot1 * (nn(hot1.astype(BF), before) + ahead), axis=0, keepdims=True)
    line = iota((8, T), 0)
    mine = jnp.where(line == 0, ids_ref[0:1].astype(F32) * CAP + rank0, 0.0)
    mine = jnp.where(line == 1, ids_ref[1:2].astype(F32) * CAP + rank1, mine)
    mine = jnp.where(line == 2, gates_ref[0:1], mine)
    meta[0, 0:8] = jnp.where(line == 3, gates_ref[1:2], mine)

    pl.semaphore_wait(barrier, len(peers))
    wires = Wires(send, recv)

    def cols(q):
        return pl.ds(Q * q, Q)

    def z_own(u):
        a, q = u
        for h in range(2):
            for side in range(2):
                wires.start(
                    ("z", u, side, h),
                    zb.at[a, pl.ds(64 * h, 64), cols(q)],
                    zb.at[a, pl.ds(256 + T * side + 64 * h, 64), cols(q)],
                    z_at(1 - 2 * side),
                )

    def z_forward(u, d):
        a, q = u
        for h in range(2):
            for side in range(2):
                wires.arrived(("z", u, side, 2 * (d - 1) + h))
                src = zb.at[a, pl.ds(256 * d + T * side + 64 * h, 64), cols(q)]
                if d < 3:
                    dst = zb.at[a, pl.ds(256 * (d + 1) + T * side + 64 * h, 64), cols(q)]
                    wires.start(("z", u, side, 2 * d + h), src, dst, z_at(1 - 2 * side))
                elif side == h:
                    dst = zb.at[a, pl.ds(T + 64 * h, 64), cols(q)]
                    wires.start(("z", u, side, 6), src, dst, z_at(1 - 2 * side))

    def z_end(u):
        for side in range(2):
            wires.arrived(("z", u, side, 6))

    def z_left(u):
        for side in range(2):
            for m in range(7):
                wires.left(("z", u, side, m))

    def targets(g, k):
        return jnp.concatenate(
            [meta[0, pl.ds(16 * g + k, 1)], meta[0, pl.ds(16 * g + 8 + k, 1)]], axis=1
        )

    def prepare(g):
        first, second = codes[...] == targets(g, 0), codes[...] == targets(g, 1)
        sel[g] = jnp.where(first | second, 1.0, 0.0).astype(BF)

    def prepare_gates(g):
        first, second = codes[...] == targets(g, 0), codes[...] == targets(g, 1)
        gate = jnp.where(first, targets(g, 2), jnp.where(second, targets(g, 3), 0.0))
        high = gate.astype(BF)
        low = (gate - high.astype(F32)).astype(BF)
        eye = jnp.where(iota((192, 192), 0) == iota((192, 192), 1), 1.0, 0.0).astype(BF)
        gsel[g, 0] = tn(high, eye).astype(BF)
        gsel[g, 1] = tn(low, eye).astype(BF)

    def select(u, g):
        a, q = u
        got = nn(sel[g], zb[a, pl.ds(256 * g, 256), cols(q)]).astype(BF)
        xsl[a, pl.ds(PAIR * g, PAIR), cols(q)] = got[0:PAIR]
        xst[a, g, pl.ds(PAIR, 3 * PAIR), cols(q)] = got[PAIR:]
        for j in range(1, 4):
            wires.start(
                ("x", u, j, g),
                xst.at[a, g, pl.ds(PAIR * j, PAIR), cols(q)],
                xsl.at[a, pl.ds((4 * j + g) * PAIR, PAIR), cols(q)],
                x_at(j),
            )

    def block(o):
        return pl.ds(ROWS * o, ROWS)

    def compact(u):
        a, q = u
        for j in range(1, 4):
            for g in range(4):
                wires.left(("x", u, j, g))
            if q == 1:
                pl.semaphore_signal(free.at[a], inc=1, device_id=x_at(j), device_id_type=MESH)
        for g in (1, 2, 3, 0):
            for j in range(1, 4):
                wires.arrived(("x", u, j, g))
        rows[a, 0:ROWS, cols(q)] = nn(pick[...], xsl[a, :, cols(q)]).astype(BF)
        wires.start(
            ("e", u, 0), rows.at[a, block(0), cols(q)], rows.at[a, block(1), cols(q)], sibling
        )

    def rows_to_mate(u):
        a, q = u
        wires.start(
            ("e", u, 1), rows.at[a, block(0), cols(q)], rows.at[a, block(2), cols(q)], row_mate
        )

    def pass_rows(u):
        a, q = u
        wires.arrived(("e", u, 1))
        wires.start(
            ("e", u, 2), rows.at[a, block(2), cols(q)], rows.at[a, block(3), cols(q)], sibling
        )

    def rows_here(a, k):
        for q in range(2):
            wires.arrived(("e", (a, q), 2 * k))

    def forward(k):
        here = pl.ds(2 * ROWS * k, 2 * ROWS)
        rows_here(RES, k)

        @pl.loop(0, HID // NT)
        def _(i):
            tile = pl.ds(pl.multiple_of(i * NT, NT), NT)
            v = nn(rows[RES, here], wi[:, tile])
            inner = jnp.tanh(coeff * (v + cubic * v * v * v))
            act[here, tile] = (0.5 * v * (1.0 + inner)).astype(BF)
            slope[here, tile] = 0.5 * (1.0 + inner) + 0.5 * v * (
                1.0 - inner * inner
            ) * coeff * (1.0 + 3.0 * cubic * v * v)

    def backward(k):
        here = pl.ds(2 * ROWS * k, 2 * ROWS)
        rows_here(GRAD, k)

        @pl.loop(0, HID // NT)
        def _(i):
            tile = pl.ds(pl.multiple_of(i * NT, NT), NT)
            got = nt(rows[GRAD, here], wo[tile, :])
            act[here, tile] = (got * slope[here, tile]).astype(BF)

    def rows_left(a):
        for q in range(2):
            for k in range(3):
                wires.left(("e", (a, q), k))

    def result(q, k):
        here = pl.ds(2 * ROWS * k, 2 * ROWS)

        @pl.loop(0, Q // NT)
        def _(i):
            tile = pl.ds(pl.multiple_of(Q * q + i * NT, NT), NT)
            rows[RES, here, tile] = nn(
                act[here, :], wo[:, tile]
            ).astype(BF)

    def input_grad(q, k):
        here = pl.ds(2 * ROWS * k, 2 * ROWS)

        @pl.loop(0, Q // NT)
        def _(i):
            tile = pl.ds(pl.multiple_of(Q * q + i * NT, NT), NT)
            rows[GRAD, here, tile] = nt(
                act[here, :], wi[tile, :]
            ).astype(BF)

    def partial_sums(u, make):
        a, q = u
        for k in (1, 0):
            make(q, k)
            wires.start(
                ("f", u, 2 * k),
                rows.at[a, block(2 * k + 1), cols(q)],
                fr.at[a, 2 * k, :, cols(q)],
                sibling,
            )

    def to_mate(u):
        a, q = u
        wires.arrived(("f", u, 2))
        rows[a, block(2), cols(q)] = (
            rows[a, block(2), cols(q)].astype(F32) + fr[a, 2, :, cols(q)].astype(F32)
        ).astype(BF)
        wires.start(("f", u, 1), rows.at[a, block(2), cols(q)], fr.at[a, 1, :, cols(q)], row_mate)

    def give_back(u):
        a, q = u
        for k in range(2):
            wires.arrived(("f", u, k))
        z_left(u)
        total = rows[a, block(0), cols(q)].astype(F32)
        for k in range(2):
            total = total + fr[a, k, :, cols(q)].astype(F32)
        zb[a, pl.ds(256, ROWS), cols(q)] = total.astype(BF)
        if q == 0:
            pl.semaphore_wait(free.at[a], 3)
        got = nn(pick_t[...], zb[a, pl.ds(256, ROWS), cols(q)]).astype(BF)
        for g in range(4):
            xst[a, g, 0:PAIR, cols(q)] = got[PAIR * g : PAIR * (g + 1)]
        xsl[a, pl.ds(4 * PAIR, 12 * PAIR), cols(q)] = got[4 * PAIR :]
        for g in (0, 3, 2, 1):
            slots_back(u, g)

    def slots_back(u, g):
        a, q = u
        for j in range(1, 4):
            wires.start(
                ("r", u, j, g),
                xsl.at[a, pl.ds((4 * j + g) * PAIR, PAIR), cols(q)],
                xst.at[a, g, pl.ds(PAIR * j, PAIR), cols(q)],
                x_at(-j),
            )

    def gathered(u, g):
        a, q = u
        for j in range(1, 4):
            wires.arrived(("r", u, j, g))
        got = xst[a, g, :, cols(q)]
        return nn(gsel[g, 0], got) + nn(gsel[g, 1], got)

    def z_back(u, side, m, src, g, h):
        a, q = u
        dst = pb.at[a, pl.ds(256 * g + T * side + 64 * h, 64), cols(q)]
        wires.start(("b", u, side, m), src, dst, z_at(2 * side - 1))

    def reduce_first(u):
        a, q = u
        got = gathered(u, 0)
        own[a, :, cols(q)] = got[0:T]
        zb[a, pl.ds(512, T), cols(q)] = got[T:].astype(BF)
        for side in range(2):
            z_back(u, side, 0, zb.at[a, pl.ds(512 + 64 * side, 64), cols(q)], 3, side)

    def reduce_next(u, g):
        a, q = u
        part[...] = gathered(u, g)
        order = ((0, 1), (1, 0), (0, 0), (1, 1)) if g == 3 else ((0, 0), (1, 0), (0, 1), (1, 1))
        for side, h in order:
            at = T * side + 64 * h
            value = part[at : at + 64]
            if g < 3 or side == h:
                wires.arrived(("b", u, side, 5 - 2 * g + h if g < 3 else 0))
                value = value + pb[a, pl.ds(256 * g + at, 64), cols(q)].astype(F32)
            pb[a, pl.ds(256 * g + at, 64), cols(q)] = value.astype(BF)
            src = pb.at[a, pl.ds(256 * g + at, 64), cols(q)]
            z_back(u, side, 7 - 2 * g + h, src, g - 1, h)

    def reduce_last(u):
        a, q = u
        for h in range(2):
            for side in range(2):
                wires.arrived(("b", u, side, 5 + h))
        return (
            own[a, :, cols(q)]
            + pb[a, 0:T, cols(q)].astype(F32)
            + pb[a, T:256, cols(q)].astype(F32)
        )

    r0, r1, g0, g1 = (RES, 0), (RES, 1), (GRAD, 0), (GRAD, 1)

    z_own(r0)
    for k in range(1, 8):
        wires.start(("mz", k), meta.at[0, pl.ds(0, 8)], meta.at[0, pl.ds(8 * Z_SLOT[k], 8)], z_at(k))
    wires.start(("w", 0), wi_ref.at[0], wi.at[:, pl.ds(SH, SH)], weight_mate)

    def more_weights(q):
        wires.start(
            ("w", 1 + q), wo_ref.at[0, :, cols(q)], wo.at[pl.ds(SH, SH), cols(q)], weight_mate
        )

    spot = iota((PAIR, 256), 0)
    spot = jnp.where(spot >= CAP, spot - CAP + 1024, spot)
    spot = spot - jnp.where(iota((PAIR, 256), 1) >= T, 1024, 0)
    spot = jnp.where((spot >= 0) & (spot < CAP), spot, -65536).astype(F32)
    for j in range(4):
        first = (z * 4 + lax.rem(x + j, 4)) * CAP
        codes[pl.ds(PAIR * j, PAIR)] = spot + first.astype(F32)
    for k in range(1, 8):
        wires.arrived(("mz", k))
    for j in range(1, 4):
        wires.start(("mx", j), meta.at[0], meta.at[j], x_at(j))

    z_forward(r0, 1)
    z_own(r1)
    prepare(1)
    select(r0, 1)
    z_forward(r0, 2)
    prepare(2)
    select(r0, 2)
    z_forward(r1, 1)
    select(r1, 1)
    prepare(3)
    prepare(0)
    z_forward(r0, 3)
    select(r0, 3)

    for j in range(1, 4):
        wires.arrived(("mx", j))
    marks = meta[...].reshape(256, T)
    low = (me_e * CAP).astype(F32)
    named = (marks >= low) & (marks < low + CAP) & ((iota((256, T), 0) & 7) < 2)
    named = jnp.where(named, 1.0, 0.0).astype(BF)
    counts = nt(jnp.ones((8, T), BF), named).astype(BF)
    begin = (iota((256, N_SLOT), 0) >> 3) * CAP
    slot = iota((256, N_SLOT), 1)
    inside = (slot >= begin) & (slot < begin + CAP)
    filled = nn(counts, jnp.where(inside, 1.0, 0.0).astype(BF))
    offset = nn(counts, jnp.where(slot >= begin + CAP, 1.0, 0.0).astype(BF))
    slot = iota((8, N_SLOT), 1).astype(F32)
    rank = slot - CAP * jnp.floor((slot + 0.5) * (1.0 / CAP))
    place = jnp.where(rank < filled, offset + rank, -1.0)
    pick[...] = jnp.where(iota((ROWS, N_SLOT), 0).astype(F32) == place[0:1], 1.0, 0.0).astype(BF)

    z_forward(r1, 2)
    z_own(g0)
    select(r1, 2)
    z_end(r0)
    select(r0, 0)
    z_forward(r1, 3)
    select(r1, 3)
    more_weights(0)
    compact(r0)
    rows_to_mate(r0)
    z_forward(g0, 1)
    z_own(g1)
    select(g0, 1)
    z_end(r1)
    select(r1, 0)
    eye = jnp.where(iota((ROWS, ROWS), 0) == iota((ROWS, ROWS), 1), 1.0, 0.0).astype(BF)
    pick_t[...] = tn(pick[...], eye).astype(BF)
    prepare_gates(0)
    prepare_gates(1)
    z_forward(g0, 2)
    select(g0, 2)
    compact(r1)
    rows_to_mate(r1)
    z_forward(g1, 1)
    select(g1, 1)
    pass_rows(r0)
    for copy in local:
        copy.wait()
    wires.arrived(("w", 0))
    forward(0)
    z_forward(g0, 3)
    select(g0, 3)
    more_weights(1)
    prepare_gates(2)
    prepare_gates(3)
    z_forward(g1, 2)
    select(g1, 2)
    pass_rows(r1)
    z_end(g0)
    select(g0, 0)
    forward(1)
    wires.arrived(("w", 1))
    rows_left(RES)
    partial_sums(r0, result)
    z_forward(g1, 3)
    select(g1, 3)
    to_mate(r0)
    compact(g0)
    rows_to_mate(g0)
    z_end(g1)
    select(g1, 0)
    wires.arrived(("w", 2))
    partial_sums(r1, result)
    compact(g1)
    rows_to_mate(g1)
    give_back(r0)
    to_mate(r1)
    pass_rows(g0)
    backward(0)
    reduce_first(r0)
    reduce_next(r0, 3)
    pass_rows(g1)
    backward(1)
    rows_left(GRAD)
    partial_sums(g0, input_grad)
    give_back(r1)
    reduce_next(r0, 2)
    to_mate(g0)
    partial_sums(g1, input_grad)
    reduce_next(r0, 1)
    reduce_first(r1)
    to_mate(g1)
    out_ref[:, cols(0)] = hid[:, cols(0)] + reduce_last(r0)
    reduce_next(r1, 3)
    give_back(g0)
    reduce_next(r1, 2)
    reduce_next(r1, 1)
    reduce_first(g0)
    give_back(g1)
    reduce_next(g0, 3)
    out_ref[:, cols(1)] = hid[:, cols(1)] + reduce_last(r1)
    reduce_first(g1)
    reduce_next(g0, 2)
    reduce_next(g1, 3)
    reduce_next(g0, 1)
    reduce_next(g1, 2)
    own[GRAD, :, cols(0)] = reduce_last(g0)
    reduce_next(g1, 1)

    inverse = inv[...]
    hid[...] = hid[...] * inverse
    first = own[GRAD, :, cols(0)] * gain[:, 0:Q]
    mean = jnp.sum(first * hid[:, cols(0)], axis=-1, keepdims=True)
    own[GRAD, :, cols(0)] = inverse * first + zb[GRAD, 0:T, cols(0)].astype(F32)
    second = reduce_last(g1) * gain[:, Q:D]
    mean = (mean + jnp.sum(second * hid[:, cols(1)], axis=-1, keepdims=True)) * (1.0 / D)
    own[GRAD, :, cols(1)] = inverse * second + zb[GRAD, 0:T, cols(1)].astype(F32)
    sum_grad = own[GRAD] - hid[...] * (inverse * mean)

    total = jnp.sum(sum_grad * ctl[...].astype(F32), axis=0, keepdims=True)
    for base, here, others in ((0, y * 4 + x, near), (16, z * 2 + c, far)):
        gb[base + here] = total
        for k, other in enumerate(others):
            wires.start(("g", base, k), gb.at[base + here], gb.at[base + here], other)
        if base == 0:
            sg_ref[...] = sum_grad
        for k in range(len(others)):
            wires.arrived(("g", base, k))
        total = gb[base]
        for k in range(1, 16):
            total = total + gb[base + k]
    gs_ref[...] = total.reshape(D)
    wires.finish()


def body(
    latents, control, control_scale, norm_gain, expert_ids, gate_weights, expert_in, expert_out, out_grad
):
    vmem = pl.BlockSpec(memory_space=pltpu.VMEM)
    hbm = pl.BlockSpec(memory_space=pl.ANY)
    output, sum_grad, grad_scale = pl.pallas_call(
        kernel,
        out_shape=(
            jax.ShapeDtypeStruct((T, D), F32),
            jax.ShapeDtypeStruct((T, D), F32),
            jax.ShapeDtypeStruct((D,), F32),
        ),
        in_specs=[vmem] * 2 + [hbm] * 3 + [vmem] * 2 + [hbm] * 2,
        out_specs=(vmem,) * 3,
        scratch_shapes=[
            pltpu.VMEM((2, 4 * 256, D), BF),
            pltpu.VMEM((2, 4, 4 * PAIR, D), BF),
            pltpu.VMEM((2, N_SLOT, D), BF),
            pltpu.VMEM((2, 4 * ROWS, D), BF),
            pltpu.VMEM((D, HID), BF),
            pltpu.VMEM((HID, D), BF),
            pltpu.VMEM((4 * ROWS, HID), BF),
            pltpu.VMEM((4 * ROWS, HID), F32),
            pltpu.VMEM((2, 3, ROWS, D), BF),
            pltpu.VMEM((2, 4 * 256, D), BF),
            pltpu.VMEM((2, T, D), F32),
            pltpu.VMEM((256, Q), F32),
            pltpu.VMEM((4 * PAIR, 256), F32),
            pltpu.VMEM((4, 4 * PAIR, 256), BF),
            pltpu.VMEM((4, 2, 256, 4 * PAIR), BF),
            pltpu.VMEM((ROWS, N_SLOT), BF),
            pltpu.VMEM((N_SLOT, ROWS), BF),
            pltpu.VMEM((4, 64, T), F32),
            pltpu.VMEM((T, D), F32),
            pltpu.VMEM((T, 1), F32),
            pltpu.VMEM((T, D), BF),
            pltpu.VMEM((T, D), BF),
            pltpu.VMEM((32, 1, D), F32),
            pltpu.SemaphoreType.DMA((N_COPIES,)),
            pltpu.SemaphoreType.DMA((N_COPIES,)),
            pltpu.SemaphoreType.DMA((5,)),
            pltpu.SemaphoreType.REGULAR((2,)),
        ],
        compiler_params=pltpu.CompilerParams(
            collective_id=0, has_side_effects=True, vmem_limit_bytes=63 * 1024 * 1024
        ),
    )(
        expert_ids.T, gate_weights.T, latents, control, out_grad, control_scale, norm_gain,
        expert_in, expert_out,
    )
    return output.astype(BF), sum_grad.astype(BF), (sum_grad * control_scale).astype(BF), grad_scale


def solution(mesh):
    return jax.shard_map(
        body,
        mesh=mesh,
        in_specs=(
            P(("seq", "expert"), None),
            P(("seq", "expert"), None),
            P(),
            P(),
            P(("seq", "expert"), None),
            P(("seq", "expert"), None),
            P("expert", None, "seq"),
            P("expert", "seq", None),
            P(("seq", "expert"), None),
        ),
        out_specs=(
            P(("seq", "expert"), None),
            P(("seq", "expert"), None),
            P(("seq", "expert"), None),
            P(),
        ),
        check_vma=False,
    )
```
